128 devices in a mesh: lat: 4 (over y), lon: 32 (over x, z, core).
Axes of the slice: x: 4, y: 4, z: 4, core: 2. Of those that a mesh axis runs over, the one named last changes fastest.
Arguments:
- state: bfloat16 [64, 128, 12288], P(None, 'lat', 'lon'), may hold values from -6 to 6
- forcing: bfloat16 [64, 128, 12288], P(None, 'lat', 'lon'), may hold values from -6 to 6
- conv_weight: bfloat16 [9, 64, 64], replicated, may hold values from -0.25 to 0.25
- w_first: bfloat16 [128, 512], replicated, may hold values from -0.5 to 0.5
- b_first: float32 [512], replicated, may hold values from -3 to 3
- w_second: bfloat16 [512, 512], replicated, may hold values from -0.25 to 0.25
- b_second: float32 [512], replicated, may hold values from -3 to 3
- w_third: bfloat16 [512, 512], replicated, may hold values from -0.25 to 0.25
- b_third: float32 [512], replicated, may hold values from -3 to 3
- w_final: bfloat16 [512, 128], replicated, may hold values from -0.25 to 0.25
- b_final: float32 [128], replicated, may hold values from -3 to 3
- active: int32 [128, 12288], P('lat', 'lon'), may hold values from 0 to 1
- owner: int32 [128, 12288], P('lat', 'lon'), may hold values from 0 to 31, as said below
- slot: int32 [128, 12288], P('lat', 'lon'), may hold values from 0 to 255, as said below
- source: int32 [4, 32, 8192], P('lat', 'lon'), may hold values from 0 to 12288, as said below
Outputs:
- new_state: bfloat16 [64, 128, 12288], P(None, 'lat', 'lon')
- owned: bfloat16 [64, 4, 32, 32, 256], P(None, 'lat', 'lon')
The draws below stay inside these ranges and needn't reach their ends.
Inputs may be any that keep to these rules, and one draw needn't show every extreme that they name: Only cells with active = 1 are owned; owner names a device of the same lat index. Among the active cells of one device the pairs (owner, slot) are distinct, and the slots used for one owner are 0 up to their count minus one. In every lat index some device hands exactly 256 columns to an owner, and every owner receives exactly 4096 columns from the devices of its lat index together. source[r, s, owner*256+slot] is the cell number of the active cell of tile (r, s) with that owner and slot, and every other entry is 12288.
All inputs are finite; a program needn't handle non-finite values.
Results may differ from the reference program's by a relative error of at most 0.0052.
Values may be sent and summed in bfloat16 or wider, within the bound.
No kernel may reach another device: no remote copies, remote signals or barrier semaphores. Data moves between devices by JAX's collectives and lax.ppermute only.
A program may use at most 128 MiB of HBM per device.

```python
import jax
import jax.numpy as jnp
from jax import lax

C = 64
FORC = 64
HID = 512
PIN = 128
TLAT = 32
TLON = 384
CAP = 256
NLAT = 128
NLON = 12288
N_LAT = 4
N_LON = 32


def cell_layout(key):
    devices_all = N_LAT * N_LON
    cells = TLAT * TLON
    half = N_LON // 2
    key_perm, key_order, key_start, key_part = jax.random.split(key, 4)
    perms = jax.vmap(lambda sub: jax.random.permutation(sub, cells))(jax.random.split(key_perm, devices_all))
    orders = jax.vmap(lambda sub: jax.random.permutation(sub, N_LON))(jax.random.split(key_order, N_LAT))
    firsts = jax.random.randint(key_start, (N_LAT, 1, N_LON), 0, half)
    partial_count = jax.random.randint(key_part, (N_LAT, 1, N_LON), 1, CAP + 1)
    rank = jnp.arange(N_LON, dtype=jnp.int32)[None, :, None] - firsts
    middle = (rank >= 1) & (rank < half)
    by_rank = jnp.where(rank == 0, partial_count, jnp.where(middle, CAP, jnp.where(rank == half, CAP - partial_count, 0)))
    by_rank = by_rank.astype(jnp.int32)
    counts = jax.vmap(lambda order, table: jnp.zeros_like(table).at[order].set(table))(orders, by_rank)
    counts = counts.reshape(devices_all, N_LON)
    positions = jnp.arange(cells)
    own_pos = positions // CAP % N_LON
    slot_pos = positions % CAP

    def place(perm, count):
        live = ((positions < N_LON * CAP) & (slot_pos < count[own_pos])).astype(jnp.int32)
        blank = jnp.zeros((cells,), jnp.int32)
        anchor = jnp.where(live[:N_LON * CAP] == 1, perm[:N_LON * CAP], cells).astype(jnp.int32)
        return (blank.at[perm].set(live), blank.at[perm].set(own_pos.astype(jnp.int32)), blank.at[perm].set(slot_pos.astype(jnp.int32)), anchor)
    act, own, slt, anchor = jax.vmap(place)(perms, counts)

    def grid(values):
        return values.reshape(N_LAT, N_LON, TLAT, TLON).transpose(0, 2, 1, 3).reshape(N_LAT * TLAT, N_LON * TLON)
    return (grid(act), grid(own), grid(slt), anchor.reshape(N_LAT, N_LON, N_LON * CAP))


def draw_active(key, part):
    return cell_layout(key)[0]


def draw_owner(key, part):
    return cell_layout(key)[1]


def draw_slot(key, part):
    return cell_layout(key)[2]


def draw_source(key, part):
    return cell_layout(key)[3]


def level_of(key, extent, cuts, smallest, largest):
    factor_of, own = 1.0, jax.random.fold_in(key, 6)
    for dim, parts in cuts:
        heights = jnp.exp(jax.random.uniform(jax.random.fold_in(own, dim), (parts,), jnp.float32, smallest / len(cuts), largest / len(cuts)))
        factor_of = factor_of * jnp.repeat(heights, extent[dim] // parts).reshape([-1 if axis == dim else 1 for axis in range(len(extent))])
    return factor_of


def scatter_about(key, extent, scale, reach, cuts=(), held_as=jnp.bfloat16):
    drawn = scale * jax.random.normal(key, extent, jnp.float32)
    if cuts:
        drawn = drawn * level_of(key, extent, cuts, -0.22, 0.18)
    return jnp.clip(drawn, -reach, reach).astype(held_as)


def setup_inputs(seed: int = 0) -> dict:
    splits = jax.random.split(jax.random.key(seed), 16)
    state = scatter_about(splits[0], (C, NLAT, NLON), 1.0, 6.0, ((1, 4), (2, 32)))
    forcing = scatter_about(splits[1], (FORC, NLAT, NLON), 1.0, 6.0, ((1, 4), (2, 32)))
    conv_weight = scatter_about(splits[2], (9, C, C), (9 * C) ** -0.5, 0.25)
    w_first = scatter_about(splits[3], (PIN, HID), PIN ** -0.5, 0.5)
    b_first = scatter_about(splits[4], (HID,), 0.5, 3.0, (), jnp.float32)
    w_second = scatter_about(splits[5], (HID, HID), HID ** -0.5, 0.25)
    b_second = scatter_about(splits[6], (HID,), 0.5, 3.0, (), jnp.float32)
    w_third = scatter_about(splits[7], (HID, HID), HID ** -0.5, 0.25)
    b_third = scatter_about(splits[8], (HID,), 0.5, 3.0, (), jnp.float32)
    w_final = scatter_about(splits[9], (HID, 2 * C), HID ** -0.5, 0.25)
    b_final = scatter_about(splits[10], (2 * C,), 0.5, 3.0, (), jnp.float32)
    active = draw_active(jax.random.fold_in(splits[15], 71), 0)
    owner = draw_owner(jax.random.fold_in(splits[15], 71), 0)
    slot = draw_slot(jax.random.fold_in(splits[15], 71), 0)
    source = draw_source(jax.random.fold_in(splits[15], 71), 0)
    return {"state": state, "forcing": forcing, "conv_weight": conv_weight, "w_first": w_first, "b_first": b_first, "w_second": w_second, "b_second": b_second, "w_third": w_third, "b_third": b_third, "w_final": w_final, "b_final": b_final, "active": active, "owner": owner, "slot": slot, "source": source}


def column_net(inputs, layers):
    hidden = inputs
    for matrix, shift in layers[:-1]:
        pre = jnp.einsum('fh,fn->hn', matrix.astype(jnp.float32), hidden.astype(jnp.float32)) + shift[:, None]
        hidden = jax.nn.gelu(pre).astype(jnp.bfloat16)
    matrix, shift = layers[-1]
    return jnp.einsum('fh,fn->hn', matrix.astype(jnp.float32), hidden.astype(jnp.float32)) + shift[:, None]


def dynamics(state, conv_weight):
    padded = jnp.pad(state, ((0, 0), (1, 1), (0, 0)))
    padded = jnp.concatenate([padded[:, :, -1:], padded, padded[:, :, :1]], axis=2)
    weights = conv_weight.astype(jnp.float32)

    def block(start):
        piece = lax.dynamic_slice_in_dim(padded, start, TLAT + 2, 1).astype(jnp.float32)
        total = jnp.zeros((C, TLAT, NLON), jnp.float32)
        for tap in range(9):
            row_off, col_off = tap // 3, tap % 3
            total = total + jnp.einsum('oc,cyx->oyx', weights[tap], piece[:, row_off:row_off + TLAT, col_off:col_off + NLON])
        return total

    starts = (jnp.arange(N_LAT) * TLAT).astype(jnp.int32)
    blocks = lax.map(block, starts)
    return blocks.transpose(1, 0, 2, 3).reshape(C, NLAT, NLON)


def to_tiles(field):
    lead = field.shape[0]
    return field.reshape(lead, N_LAT, TLAT, N_LON, TLON).transpose(1, 3, 0, 2, 4).reshape(N_LAT * N_LON, lead, TLAT * TLON)


def reference(state, forcing, conv_weight, w_first, b_first, w_second, b_second, w_third, b_third, w_final, b_final, active, owner, slot, source):
    conv = dynamics(state, conv_weight)
    dyn = (state.astype(jnp.float32) + conv).astype(jnp.bfloat16)
    columns = to_tiles(jnp.concatenate([dyn, forcing], axis=0))
    act_t = to_tiles(active[None])[:, 0]
    own_t = to_tiles(owner[None])[:, 0]
    slot_t = to_tiles(slot[None])[:, 0]
    src_t = source.reshape(N_LAT * N_LON, N_LON * CAP)
    layers = ((w_first, b_first), (w_second, b_second), (w_third, b_third), (w_final, b_final))
    slots_all = N_LON * CAP
    cells = TLAT * TLON

    def one_tile(pieces):
        cols, act, own, slt, src = pieces
        padded = jnp.concatenate([cols, jnp.zeros((PIN, 1), jnp.bfloat16)], axis=1)
        buffer = padded[:, src]
        valid = (src < cells).astype(jnp.float32)
        phys = column_net(buffer, layers)
        tend = phys[:C].astype(jnp.bfloat16)
        place = jnp.where(act == 1, own * CAP + slt, 0).astype(jnp.int32)
        tend_cells = tend[:, place].astype(jnp.float32) * act.astype(jnp.float32)[None, :]
        diag = (phys[C:] * valid[None, :]).astype(jnp.bfloat16)
        return tend_cells, diag

    tend_cells, diag = lax.map(one_tile, (columns, act_t, own_t, slot_t, src_t))
    tend_grid = tend_cells.reshape(N_LAT, N_LON, C, TLAT, TLON).transpose(2, 0, 3, 1, 4).reshape(C, NLAT, NLON)
    new_state = (dyn.astype(jnp.float32) + tend_grid).astype(jnp.bfloat16)
    owned = diag.reshape(N_LAT, N_LON, C, N_LON, CAP).transpose(2, 0, 3, 1, 4)
    return new_state, owned
```

```python
import functools

import jax
import jax.numpy as jnp
from jax import lax
from jax.experimental import pallas as pl
from jax.experimental.pallas import tpu as pltpu
from jax.sharding import PartitionSpec as P

K0 = 0.7978845608028654
K1 = K0 * 0.044715
SUB = 128
GROUP = 4


def half_gelu(y):
    t = jnp.tanh(y * (2.0 * K0 + (8.0 * K1) * (y * y)))
    return y + y * t


def active_blocks(src, table, cells, blocks):
    def scan(b, n):
        table[n] = b
        return n + (src[b * SUB] < cells).astype(jnp.int32)

    count = lax.fori_loop(0, blocks, scan, jnp.int32(0))
    last = table[jnp.maximum(count - 1, 0)]
    last = jnp.where(count > 0, last, 0)
    for extra in range(GROUP):
        table[count + extra] = last
    return count


def columns_kernel(
    src, s_ref, e_ref, top_ref, bot_ref, f_ref, cw_ref, w1_ref, b1_ref, w2_ref, b2_ref,
    w3_ref, b3_ref, w4_ref, b4_ref, vsrc_ref,
    dyn_ref, tend_ref, send_ref,
    ext, feats, xbuf, w1h, w2h, w3h, table,
):
    rows, chans, cols = s_ref.shape
    cells = rows * cols
    blocks = vsrc_ref.shape[0]
    wide = cols + 128
    ext[0] = top_ref[...]
    ext[rows + 1] = bot_ref[...]
    ext[1 : rows + 1, :, :cols] = s_ref[...]
    ext[1 : rows + 1, :, cols:] = e_ref[...]
    feats[cells : cells + 8, :] = jnp.zeros((8, 2 * chans), jnp.float32)
    w1h[...] = w1_ref[...] * jnp.bfloat16(0.5)
    w2h[...] = w2_ref[...] * jnp.bfloat16(0.5)
    w3h[...] = w3_ref[...] * jnp.bfloat16(0.5)
    send_ref[...] = jnp.zeros(send_ref.shape, send_ref.dtype)

    def conv_row(y, carry):
        x = ext[pl.ds(y, 3)].reshape(3 * chans, wide)
        p = jnp.dot(cw_ref[...], x, preferred_element_type=jnp.float32)
        total = (
            s_ref[y].astype(jnp.float32)
            + p[chans : 2 * chans, :cols]
            + pltpu.roll(p[:chans], 1, 1)[:, :cols]
            + pltpu.roll(p[2 * chans :], wide - 1, 1)[:, :cols]
        )
        dyn = total.astype(jnp.bfloat16)
        dyn_ref[y] = dyn
        both = jnp.concatenate([dyn.astype(jnp.float32), f_ref[y].astype(jnp.float32)], axis=0)
        feats[pl.ds(pl.multiple_of(y * cols, 128), cols), :] = both.T
        return carry

    lax.fori_loop(0, rows, conv_row, 0)

    count = active_blocks(src, table, cells, blocks)

    def group(g, carry):
        for j in range(GROUP):
            base = table[g * GROUP + j] * SUB

            def fetch(i, c, base=base, j=j):
                for r in range(16):
                    at = src[base + i * 16 + r]
                    xbuf[pl.ds(j * SUB + i * 16 + r, 1), :] = feats[pl.ds(at, 1), :]
                return c

            lax.fori_loop(0, SUB // 16, fetch, 0)
        h = xbuf[...].astype(jnp.bfloat16)
        for w, b in ((w1h, b1_ref), (w2h, b2_ref), (w3h, b3_ref)):
            pre = jnp.dot(h, w[...], preferred_element_type=jnp.float32) + b[...] * 0.5
            h = half_gelu(pre).astype(jnp.bfloat16)
        out = jnp.dot(h, w4_ref[...], preferred_element_type=jnp.float32) + b4_ref[...]
        for j in range(GROUP):
            blk = table[g * GROUP + j]
            part = out[j * SUB : (j + 1) * SUB]
            tend_ref[pl.ds(pl.multiple_of(blk * SUB, SUB), SUB), :] = part.astype(jnp.bfloat16)
            ok = vsrc_ref[pl.ds(blk, 1), :] < cells
            diag = jnp.where(ok, part.T[chans:], 0.0)
            send_ref[blk] = diag.astype(jnp.bfloat16)
        return carry

    lax.fori_loop(0, (count + GROUP - 1) // GROUP, group, 0)


def place_kernel(src, dyn_ref, tend_ref, new_ref, acc, rbuf, table):
    rows, chans, cols = dyn_ref.shape
    cells = rows * cols
    blocks = tend_ref.shape[0] // SUB

    acc[...] = jnp.zeros(acc.shape, jnp.float32)
    count = active_blocks(src, table, cells, blocks)

    def block(n, carry):
        base = table[n] * SUB
        rbuf[...] = tend_ref[pl.ds(pl.multiple_of(base, SUB), SUB), :].astype(jnp.float32)

        def put(i, c):
            for r in range(16):
                at = src[base + i * 16 + r]
                acc[pl.ds(at, 1), :] = rbuf[pl.ds(i * 16 + r, 1), :]
            return c

        lax.fori_loop(0, SUB // 16, put, 0)
        return carry

    lax.fori_loop(0, count, block, 0)

    def row(y, carry):
        part = acc[pl.ds(pl.multiple_of(y * cols, 128), cols), :].T[:chans]
        new_ref[y] = (dyn_ref[y].astype(jnp.float32) + part).astype(jnp.bfloat16)
        return carry

    lax.fori_loop(0, rows, row, 0)


def shift(block, axis, step, periodic):
    count = lax.axis_size(axis)
    pairs = [(i, (i + step) % count) for i in range(count) if periodic or 0 <= i + step < count]
    return lax.ppermute(block, axis, pairs)


def body(
    state, forcing, conv_weight, w_first, b_first, w_second, b_second, w_third, b_third,
    w_final, b_final, active, owner, slot, source,
):
    chans, rows, cols = state.shape
    slots = source.size
    blocks = slots // SUB
    cells = rows * cols
    hid = w_second.shape[0]
    src = source.reshape(slots)

    s = state.transpose(1, 0, 2)
    left = shift(s[:, :, cols - 1 :], "lon", 1, True)
    right = shift(s[:, :, :1], "lon", -1, True)
    f = forcing.transpose(1, 0, 2)
    cw = conv_weight.reshape(3, 3, chans, chans).transpose(1, 2, 0, 3).reshape(3 * chans, 3 * chans)
    edge = jnp.concatenate([right, jnp.zeros((rows, chans, 126), jnp.bfloat16), left], axis=2)
    top = shift(jnp.concatenate([s[-1], edge[-1]], axis=1), "lat", 1, False)
    bot = shift(jnp.concatenate([s[0], edge[0]], axis=1), "lat", -1, False)

    vmem = pl.BlockSpec(memory_space=pltpu.VMEM)
    smem = pl.BlockSpec(memory_space=pltpu.SMEM)
    dyn, tend, send = pl.pallas_call(
        columns_kernel,
        out_shape=(
            jax.ShapeDtypeStruct((rows, chans, cols), jnp.bfloat16),
            jax.ShapeDtypeStruct((slots, 2 * chans), jnp.bfloat16),
            jax.ShapeDtypeStruct((blocks, chans, SUB), jnp.bfloat16),
        ),
        in_specs=[smem] + [vmem] * 15,
        out_specs=(vmem, vmem, vmem),
        scratch_shapes=[
            pltpu.VMEM((rows + 2, chans, cols + 128), jnp.bfloat16),
            pltpu.VMEM((cells + 8, 2 * chans), jnp.float32),
            pltpu.VMEM((GROUP * SUB, 2 * chans), jnp.float32),
            pltpu.VMEM(w_first.shape, jnp.bfloat16),
            pltpu.VMEM(w_second.shape, jnp.bfloat16),
            pltpu.VMEM(w_third.shape, jnp.bfloat16),
            pltpu.SMEM((blocks + GROUP + 4,), jnp.int32),
        ],
        compiler_params=pltpu.CompilerParams(vmem_limit_bytes=48 << 20),
        cost_estimate=pl.CostEstimate(flops=10_000_000_000, bytes_accessed=8_000_000, transcendentals=8_000_000),
        name="columns",
    )(
        src, s, edge, top, bot, f, cw, w_first, b_first.reshape(1, hid), w_second,
        b_second.reshape(1, hid), w_third, b_third.reshape(1, hid), w_final,
        b_final.reshape(1, 2 * chans), src.reshape(blocks, SUB),
    )
    got = lax.all_to_all(send, "lon", split_axis=0, concat_axis=0, tiled=True)
    new = pl.pallas_call(
        place_kernel,
        out_shape=jax.ShapeDtypeStruct((rows, chans, cols), jnp.bfloat16),
        in_specs=[smem, vmem, vmem],
        out_specs=vmem,
        scratch_shapes=[
            pltpu.VMEM((cells + 8, 2 * chans), jnp.float32),
            pltpu.VMEM((SUB, 2 * chans), jnp.float32),
            pltpu.SMEM((blocks + GROUP + 4,), jnp.int32),
        ],
        compiler_params=pltpu.CompilerParams(vmem_limit_bytes=32 << 20),
        cost_estimate=pl.CostEstimate(flops=5_000_000_000, bytes_accessed=8_000_000, transcendentals=0),
        name="place",
    )(src, dyn, tend)
    new_state = new.transpose(1, 0, 2)
    owners = lax.axis_size("lon")
    halves = blocks // owners
    owned = got.reshape(owners, halves, chans, SUB).transpose(2, 0, 1, 3).reshape(chans, 1, 1, owners, halves * SUB)
    return (new_state, owned)


def solution(mesh):
    field = P(None, "lat", "lon")
    return jax.shard_map(
        body,
        mesh=mesh,
        in_specs=(field, field) + (P(),) * 9 + (P("lat", "lon"),) * 3 + (P("lat", "lon", None),),
        out_specs=(field, P(None, "lat", "lon", None, None)),
        check_vma=False,
    )
```

```python
import jax
import jax.numpy as jnp
from jax import lax
from jax.experimental import pallas as pl
from jax.experimental.pallas import tpu as pltpu
from jax.sharding import PartitionSpec as P

K0 = 0.7978845608028654
K1 = K0 * 0.044715
LANES = 128
GROUP = 512
BF = jnp.bfloat16
F32 = jnp.float32


def lane_index(rows):
    return lax.broadcasted_iota(jnp.int32, (rows, LANES), 1)


def half_gelu(y):
    t = jnp.tanh(y * (2.0 * K0 + (8.0 * K1) * (y * y)))
    return (y + y * t).astype(BF)


def edges_kernel(low_ref, high_ref, pay_ref):
    chans, rows, _ = low_ref.shape
    lane = lane_index(rows)
    acc = jnp.zeros((rows, LANES), F32)
    for c in range(chans):
        low = jnp.broadcast_to(low_ref[c].astype(F32)[:, :1], (rows, LANES))
        high = jnp.broadcast_to(high_ref[c].astype(F32)[:, LANES - 1 :], (rows, LANES))
        acc = jnp.where(lane == c, low, jnp.where(lane == chans + c, high, acc))
    pay_ref[...] = acc.astype(BF)


def halo_columns(left_ref, right_ref, chans):
    rows = left_ref.shape[0]
    pad = jnp.zeros((LANES - rows, LANES), F32)
    left = jnp.concatenate([left_ref[...].astype(F32), pad], axis=0).T[chans : 2 * chans]
    right = jnp.concatenate([right_ref[...].astype(F32), pad], axis=0).T[:chans]
    return left, right


def halo_tile(left, right, y, chans):
    lane = lane_index(chans)
    low = jnp.broadcast_to(right[:, y : y + 1], (chans, LANES))
    high = jnp.broadcast_to(left[:, y : y + 1], (chans, LANES))
    return jnp.where(lane == 0, low, jnp.where(lane == LANES - 1, high, 0.0)).astype(BF)


def rows_kernel(left_ref, right_ref, first_ref, last_ref, up_ref, down_ref):
    _, chans, cols = first_ref.shape
    rows = left_ref.shape[0]
    left, right = halo_columns(left_ref, right_ref, chans)
    up_ref[:, :cols] = first_ref[0]
    up_ref[:, cols:] = halo_tile(left, right, 0, chans)
    down_ref[:, :cols] = last_ref[0]
    down_ref[:, cols:] = halo_tile(left, right, rows - 1, chans)


def columns_kernel(
    src, s_ref, left_ref, right_ref, top_ref, bot_ref, f_ref, cw_ref, w1_ref, b1_ref, w2_ref,
    b2_ref, w3_ref, b3_ref, w4_ref, b4_ref, vsrc_ref,
    dyn_ref, tend_ref, send_ref,
    ext, feats, buf0, buf1, w1h, w2h, w3h,
):
    rows, chans, cols = s_ref.shape
    cells = rows * cols
    owners, _, cap = send_ref.shape
    slots = tend_ref.shape[0]
    wide = cols + LANES
    groups = slots // GROUP
    ext[0] = top_ref[...]
    ext[rows + 1] = bot_ref[...]
    ext[1 : rows + 1, :, :cols] = s_ref[...]
    left, right = halo_columns(left_ref, right_ref, chans)
    for y in range(rows):
        ext[y + 1, :, cols:] = halo_tile(left, right, y, chans)
    feats[cells : cells + 8, :] = jnp.zeros((8, 2 * chans), F32)

    hid = w2h.shape[0]
    half = b1_ref[...] * 0.5
    high = half.astype(BF)
    rest = half - high.astype(F32)
    mid = rest.astype(BF)
    low = (rest - mid.astype(F32)).astype(BF)
    row = lax.broadcasted_iota(jnp.int32, (LANES, hid), 0)
    w1h[:LANES] = w1_ref[...] * BF(0.5)
    w1h[LANES:] = jnp.where(
        row == 0, high.astype(F32), jnp.where(row == 1, mid.astype(F32), jnp.where(row == 2, low.astype(F32), 0.0))
    ).astype(BF)
    w2h[...] = w2_ref[...] * BF(0.5)
    w3h[...] = w3_ref[...] * BF(0.5)

    def conv_row(y, carry):
        x = ext[pl.ds(y, 3)].reshape(3 * chans, wide)
        p = jnp.dot(cw_ref[...], x, preferred_element_type=F32)
        total = (
            s_ref[y].astype(F32)
            + p[chans : 2 * chans, :cols]
            + pltpu.roll(p[:chans], 1, 1)[:, :cols]
            + pltpu.roll(p[2 * chans :], wide - 1, 1)[:, :cols]
        )
        dyn = total.astype(BF)
        dyn_ref[y] = dyn
        both = jnp.concatenate([dyn.astype(F32), f_ref[y].astype(F32)], axis=0)
        feats[pl.ds(pl.multiple_of(y * cols, LANES), cols), :] = both.T
        return carry

    lax.fori_loop(0, rows, conv_row, 0, unroll=8)

    def fetch(g, buf, start, stop):
        base = jnp.minimum(g, groups - 1) * GROUP
        for r in range(start, stop):
            buf[pl.ds(r, 1), :] = feats[pl.ds(src[base + r], 1), :]

    ones = jnp.ones((GROUP, LANES), BF)

    def net(g, buf, following):
        part = GROUP // 4
        h = jnp.concatenate([buf[...].astype(BF), ones], axis=1)
        fetch(g + 1, following, 0, part)
        h = half_gelu(jnp.dot(h, w1h[...], preferred_element_type=F32))
        fetch(g + 1, following, part, 2 * part)
        h = half_gelu(jnp.dot(h, w2h[...], preferred_element_type=F32) + b2_ref[...] * 0.5)
        fetch(g + 1, following, 2 * part, 3 * part)
        h = half_gelu(jnp.dot(h, w3h[...], preferred_element_type=F32) + b3_ref[...] * 0.5)
        fetch(g + 1, following, 3 * part, GROUP)
        out = jnp.dot(h, w4_ref[...], preferred_element_type=F32) + b4_ref[...]
        tend_ref[pl.ds(pl.multiple_of(g * GROUP, GROUP), GROUP), :] = out.astype(BF)
        flip = out.T[chans:]
        for j in range(GROUP // cap):
            o = g * (GROUP // cap) + j
            diag = jnp.where(vsrc_ref[pl.ds(o, 1), :] < cells, flip[:, j * cap : (j + 1) * cap], 0.0)
            send_ref[o] = diag.astype(BF)

    fetch(0, buf0, 0, GROUP)

    def pair(i, carry):
        net(2 * i, buf0, buf1)
        net(2 * i + 1, buf1, buf0)
        return carry

    lax.fori_loop(0, groups // 2, pair, 0)


def place_kernel(src, dyn_ref, tend_ref, new_ref, acc, rows_f32):
    rows, chans, cols = dyn_ref.shape
    slots = tend_ref.shape[0]

    acc[...] = jnp.zeros(acc.shape, F32)

    def block(n, carry):
        base = n * LANES
        rows_f32[...] = tend_ref[pl.ds(pl.multiple_of(base, LANES), LANES), :].astype(F32)
        for r in range(LANES):
            acc[pl.ds(src[base + r], 1), :] = rows_f32[pl.ds(r, 1), :]
        return carry

    lax.fori_loop(0, slots // LANES, block, 0)

    def row(y, carry):
        part = acc[pl.ds(pl.multiple_of(y * cols, LANES), cols), :].T[:chans]
        new_ref[y] = (dyn_ref[y].astype(F32) + part).astype(BF)
        return carry

    lax.fori_loop(0, rows, row, 0, unroll=4)


def owned_kernel(got_ref, out_ref, wide):
    owners, chans, cap = got_ref.shape
    for h in range(cap // LANES):
        part = slice(h * LANES, (h + 1) * LANES)
        for s in range(owners):
            wide[h, pl.ds(s, chans, stride=owners), :] = got_ref[s, :, part].astype(F32)
        for c in range(chans):
            out_ref[c, :, part] = wide[h, c * owners : (c + 1) * owners, :].astype(BF)


def shift(block, axis, step, periodic):
    count = lax.axis_size(axis)
    pairs = [(i, (i + step) % count) for i in range(count) if periodic or 0 <= i + step < count]
    return lax.ppermute(block, axis, pairs)


def body(
    state, forcing, conv_weight, w_first, b_first, w_second, b_second, w_third, b_third,
    w_final, b_final, active, owner, slot, source,
):
    chans, rows, cols = state.shape
    slots = source.size
    cells = rows * cols
    hid = w_second.shape[0]
    owners = lax.axis_size("lon")
    cap = slots // owners
    wide = cols + LANES
    src = source.reshape(slots)
    vmem = pl.BlockSpec(memory_space=pltpu.VMEM)
    smem = pl.BlockSpec(memory_space=pltpu.SMEM)

    tile = (chans, rows, LANES)
    pay = pl.pallas_call(
        edges_kernel,
        grid=(1,),
        out_shape=jax.ShapeDtypeStruct((rows, LANES), BF),
        in_specs=[
            pl.BlockSpec(tile, lambda i: (0, 0, 0)),
            pl.BlockSpec(tile, lambda i: (0, 0, cols // LANES - 1)),
        ],
        out_specs=pl.BlockSpec((rows, LANES), lambda i: (0, 0)),
        name="edges",
    )(state, state)
    left = shift(pay, "lon", 1, True)
    right = shift(pay, "lon", -1, True)
    s = state.transpose(1, 0, 2)
    f = forcing.transpose(1, 0, 2)
    cw = conv_weight.reshape(3, 3, chans, chans).transpose(1, 2, 0, 3).reshape(3 * chans, 3 * chans)
    whole = pl.BlockSpec((rows, LANES), lambda i: (0, 0))
    up, down = pl.pallas_call(
        rows_kernel,
        grid=(1,),
        out_shape=(jax.ShapeDtypeStruct((chans, wide), BF),) * 2,
        in_specs=[
            whole,
            whole,
            pl.BlockSpec((1, chans, cols), lambda i: (0, 0, 0)),
            pl.BlockSpec((1, chans, cols), lambda i: (rows - 1, 0, 0)),
        ],
        out_specs=(pl.BlockSpec((chans, wide), lambda i: (0, 0)),) * 2,
        name="rows",
    )(left, right, s, s)
    top = shift(down, "lat", 1, False)
    bot = shift(up, "lat", -1, False)

    dyn, tend, send = pl.pallas_call(
        columns_kernel,
        out_shape=(
            jax.ShapeDtypeStruct((rows, chans, cols), BF),
            jax.ShapeDtypeStruct((slots, 2 * chans), BF),
            jax.ShapeDtypeStruct((owners, chans, cap), BF),
        ),
        in_specs=[smem] + [vmem] * 16,
        out_specs=(vmem, vmem, vmem),
        scratch_shapes=[
            pltpu.VMEM((rows + 2, chans, wide), BF),
            pltpu.VMEM((cells + 8, 2 * chans), F32),
            pltpu.VMEM((GROUP, 2 * chans), F32),
            pltpu.VMEM((GROUP, 2 * chans), F32),
            pltpu.VMEM((2 * LANES, hid), BF),
            pltpu.VMEM(w_second.shape, BF),
            pltpu.VMEM(w_third.shape, BF),
        ],
        compiler_params=pltpu.CompilerParams(vmem_limit_bytes=40 << 20),
        cost_estimate=pl.CostEstimate(flops=10_000_000_000, bytes_accessed=8_000_000, transcendentals=12_000_000),
        name="columns",
    )(
        src, s, left, right, top, bot, f, cw, w_first, b_first.reshape(1, hid), w_second,
        b_second.reshape(1, hid), w_third, b_third.reshape(1, hid), w_final,
        b_final.reshape(1, 2 * chans), src.reshape(owners, cap),
    )
    got = lax.all_to_all(send, "lon", split_axis=0, concat_axis=0, tiled=True)
    new = pl.pallas_call(
        place_kernel,
        out_shape=jax.ShapeDtypeStruct((rows, chans, cols), BF),
        in_specs=[smem, vmem, vmem],
        out_specs=vmem,
        scratch_shapes=[
            pltpu.VMEM((cells + 8, 2 * chans), F32),
            pltpu.VMEM((LANES, 2 * chans), F32),
        ],
        compiler_params=pltpu.CompilerParams(vmem_limit_bytes=32 << 20),
        cost_estimate=pl.CostEstimate(flops=5_000_000_000, bytes_accessed=8_000_000, transcendentals=0),
        name="place",
    )(src, dyn, tend)
    new_state = new.transpose(1, 0, 2)
    owned = pl.pallas_call(
        owned_kernel,
        out_shape=jax.ShapeDtypeStruct((chans, owners, cap), BF),
        in_specs=[vmem],
        out_specs=vmem,
        scratch_shapes=[pltpu.VMEM((cap // LANES, chans * owners, LANES), F32)],
        compiler_params=pltpu.CompilerParams(vmem_limit_bytes=16 << 20),
        name="owned",
    )(got)
    return (new_state, owned.reshape(chans, 1, 1, owners, cap))


def solution(mesh):
    field = P(None, "lat", "lon")
    return jax.shard_map(
        body,
        mesh=mesh,
        in_specs=(field, field) + (P(),) * 9 + (P("lat", "lon"),) * 3 + (P("lat", "lon", None),),
        out_specs=(field, P(None, "lat", "lon", None, None)),
        check_vma=False,
    )
```

```python
import jax
import jax.numpy as jnp
from jax import lax
from jax.experimental import pallas as pl
from jax.experimental.pallas import tpu as pltpu
from jax.sharding import PartitionSpec as P

K0 = 0.7978845608028654
K1 = K0 * 0.044715
LANES = 128
GROUP = 512
CHUNK = 8
PITCH = 33
BF = jnp.bfloat16
F32 = jnp.float32


def lane_index(rows):
    return lax.broadcasted_iota(jnp.int32, (rows, LANES), 1)


def half_gelu(y):
    t = jnp.tanh(y * (2.0 * K0 + (8.0 * K1) * (y * y)))
    return (y + y * t).astype(BF)


def edges_kernel(low_ref, high_ref, pay_ref):
    chans, rows, _ = low_ref.shape
    lane = lane_index(rows)
    acc = jnp.zeros((rows, LANES), F32)
    for c in range(chans):
        low = jnp.broadcast_to(low_ref[c].astype(F32)[:, :1], (rows, LANES))
        high = jnp.broadcast_to(high_ref[c].astype(F32)[:, LANES - 1 :], (rows, LANES))
        acc = jnp.where(lane == c, low, jnp.where(lane == chans + c, high, acc))
    pay_ref[...] = acc.astype(BF)


def halo_columns(left_ref, right_ref, chans):
    rows = left_ref.shape[0]
    pad = jnp.zeros((LANES - rows, LANES), F32)
    left = jnp.concatenate([left_ref[...].astype(F32), pad], axis=0).T[chans : 2 * chans]
    right = jnp.concatenate([right_ref[...].astype(F32), pad], axis=0).T[:chans]
    return left, right


def halo_tile(left, right, y, chans):
    lane = lane_index(chans)
    low = jnp.broadcast_to(right[:, y : y + 1], (chans, LANES))
    high = jnp.broadcast_to(left[:, y : y + 1], (chans, LANES))
    return jnp.where(lane == 0, low, jnp.where(lane == LANES - 1, high, 0.0)).astype(BF)


def rows_kernel(left_ref, right_ref, first_ref, last_ref, up_ref, down_ref):
    _, chans, cols = first_ref.shape
    rows = left_ref.shape[0]
    left, right = halo_columns(left_ref, right_ref, chans)
    up_ref[:, :cols] = first_ref[0]
    up_ref[:, cols:] = halo_tile(left, right, 0, chans)
    down_ref[:, :cols] = last_ref[0]
    down_ref[:, cols:] = halo_tile(left, right, rows - 1, chans)


def columns_kernel(
    src, s_any, left_ref, right_ref, top_ref, bot_ref, f_any, cw_ref,
    w1_any, b1_ref, w2_any, b2_ref, w3_any, b3_ref, w4_any, b4_ref, vsrc_ref,
    dyn_any, tend_ref, send_ref,
    ext, feats, f_ref, dyn_ref, buf0, buf1, w1h, w2h, w3h, w1_ref, w2_ref, w3_ref, w4_ref,
    tend_buf, send_buf, s_sems, f_sems, dyn_sems, w_sems, tend_sems, send_sems,
):
    rows, chans, cols = f_ref.shape
    cells = rows * cols
    owners, _, cap = send_ref.shape
    slots = tend_ref.shape[0]
    groups = slots // GROUP
    wide = cols + LANES
    chunks = rows // CHUNK

    def s_load(k):
        at = k * CHUNK
        target = ext.at[pl.ds(at + 1, CHUNK), :, pl.ds(0, cols)]
        return pltpu.make_async_copy(s_any.at[pl.ds(at, CHUNK)], target, s_sems.at[k])

    def f_load(k):
        part = pl.ds(k * CHUNK, CHUNK)
        return pltpu.make_async_copy(f_any.at[part], f_ref.at[part], f_sems.at[k])

    def dyn_store(k):
        part = pl.ds(k * CHUNK, CHUNK)
        return pltpu.make_async_copy(dyn_ref.at[part], dyn_any.at[part], dyn_sems.at[k])

    for k in range(chunks):
        s_load(k).start()
        f_load(k).start()
    loads = [
        pltpu.make_async_copy(source, target, w_sems.at[k])
        for k, (source, target) in enumerate(
            ((w1_any, w1_ref), (w2_any, w2_ref), (w3_any, w3_ref), (w4_any, w4_ref))
        )
    ]
    for load in loads:
        load.start()
    ext[0] = top_ref[...]
    ext[rows + 1] = bot_ref[...]
    left, right = halo_columns(left_ref, right_ref, chans)
    for y in range(rows):
        ext[y + 1, :, cols:] = halo_tile(left, right, y, chans)
    feats[cells : cells + 8, :] = jnp.zeros((8, 2 * chans), F32)

    def conv_row(y):
        x = ext[pl.ds(y, 3)].reshape(3 * chans, wide)
        p = jnp.dot(cw_ref[...], x, preferred_element_type=F32)
        total = (
            x[chans : 2 * chans, :cols].astype(F32)
            + p[chans : 2 * chans, :cols]
            + pltpu.roll(p[:chans], 1, 1)[:, :cols]
            + pltpu.roll(p[2 * chans :], wide - 1, 1)[:, :cols]
        )
        dyn = total.astype(BF)
        dyn_ref[y] = dyn
        both = jnp.concatenate([dyn.astype(F32), f_ref[y].astype(F32)], axis=0)
        feats[pl.ds(pl.multiple_of(y * cols, LANES), cols), :] = both.T

    s_load(0).wait()

    def chunk(k, carry):
        @pl.when(k < chunks - 1)
        def _():
            s_load(jnp.minimum(k + 1, chunks - 1)).wait()

        f_load(k).wait()
        for n in range(CHUNK):
            conv_row(k * CHUNK + n)
        dyn_store(k).start()
        return carry

    lax.fori_loop(0, chunks, chunk, 0)

    for load in loads:
        load.wait()
    hid = w2h.shape[0]
    half = b1_ref[...] * 0.5
    high = half.astype(BF)
    rest = half - high.astype(F32)
    mid = rest.astype(BF)
    low = (rest - mid.astype(F32)).astype(BF)
    row = lax.broadcasted_iota(jnp.int32, (LANES, hid), 0)
    w1h[:LANES] = w1_ref[...] * BF(0.5)
    w1h[LANES:] = jnp.where(
        row == 0, high.astype(F32), jnp.where(row == 1, mid.astype(F32), jnp.where(row == 2, low.astype(F32), 0.0))
    ).astype(BF)
    w2h[...] = w2_ref[...] * BF(0.5)
    w3h[...] = w3_ref[...] * BF(0.5)

    def fetch(g, buf, start, stop):
        base = jnp.minimum(g, groups - 1) * GROUP
        for r in range(start, stop, 8):
            rows8 = feats[pl.ds(src[0, base + r], 8, stride=0), :]
            for k in range(1, 8):
                rows8 = jnp.where(sub == k, feats[pl.ds(src[0, base + r + k], 8, stride=0), :], rows8)
            buf[r : r + 8, :] = rows8

    sub = lax.broadcasted_iota(jnp.int32, (8, LANES), 0)
    ones = jnp.ones((GROUP, LANES), BF)

    each = GROUP // cap

    def outward(i):
        rows_part = pl.ds(pl.multiple_of(i * 2 * GROUP, GROUP), 2 * GROUP)
        owner_part = pl.ds(i * 2 * each, 2 * each)
        return (
            pltpu.make_async_copy(tend_buf.at[rows_part], tend_ref.at[rows_part], tend_sems.at[i]),
            pltpu.make_async_copy(send_buf.at[owner_part], send_ref.at[owner_part], send_sems.at[i]),
        )

    def net(g, buf, following):
        part = GROUP // 4
        h = jnp.concatenate([buf[...].astype(BF), ones], axis=1)
        fetch(g + 1, following, 0, part)
        h = half_gelu(jnp.dot(h, w1h[...], preferred_element_type=F32))
        fetch(g + 1, following, part, 2 * part)
        h = half_gelu(jnp.dot(h, w2h[...], preferred_element_type=F32) + b2_ref[...] * 0.5)
        fetch(g + 1, following, 2 * part, 3 * part)
        h = half_gelu(jnp.dot(h, w3h[...], preferred_element_type=F32) + b3_ref[...] * 0.5)
        fetch(g + 1, following, 3 * part, GROUP)
        out = jnp.dot(h, w4_ref[...], preferred_element_type=F32) + b4_ref[...]
        flip = out.T[chans:]
        tend_buf[pl.ds(pl.multiple_of(g * GROUP, GROUP), GROUP), :] = out.astype(BF)
        for j in range(each):
            at = pl.multiple_of((g * each + j) * cap, LANES)
            filled = vsrc_ref[:, pl.ds(at, cap)] < cells
            diag = jnp.where(filled, flip[:, j * cap : (j + 1) * cap], 0.0)
            send_buf[g * each + j] = diag.astype(BF)

    fetch(0, buf0, 0, GROUP)

    def pair(i, carry):
        net(2 * i, buf0, buf1)
        net(2 * i + 1, buf1, buf0)
        for copy in outward(i):
            copy.start()
        return carry

    lax.fori_loop(0, groups // 2, pair, 0)
    for i in range(groups // 2):
        for copy in outward(i):
            copy.wait()
    for k in range(chunks):
        dyn_store(k).wait()


def place_kernel(src, dyn_any, tend_any, new_ref, acc, rows_f32, dyn_ref, tend_ref, new_wide, sems):
    chans, rows, cols = new_ref.shape
    slots = tend_ref.shape[0]
    tend_copy = pltpu.make_async_copy(tend_any, tend_ref, sems.at[0])
    tend_copy.start()
    dyn_copy = pltpu.make_async_copy(dyn_any, dyn_ref, sems.at[1])
    dyn_copy.start()
    acc[...] = jnp.zeros(acc.shape, F32)
    tend_copy.wait()

    def block(n, carry):
        base = n * LANES
        rows_f32[...] = tend_ref[pl.ds(pl.multiple_of(base, LANES), LANES), :].astype(F32)
        for r in range(LANES):
            acc[pl.ds(src[0, base + r], 1), :] = rows_f32[pl.ds(r, 1), :]
        return carry

    lax.fori_loop(0, slots // LANES, block, 0)
    dyn_copy.wait()

    def row(y, carry):
        part = acc[pl.ds(pl.multiple_of(y * cols, LANES), cols), :].T[:chans]
        total = dyn_ref[y].astype(F32) + part
        for t in range(cols // LANES):
            new_wide[t, pl.ds(y, chans, stride=PITCH), :] = total[:, t * LANES : (t + 1) * LANES]
        return carry

    lax.fori_loop(0, rows, row, 0, unroll=4)
    for c in range(chans):
        for t in range(cols // LANES):
            part = new_wide[t, c * PITCH : c * PITCH + rows, :]
            new_ref[c, :, t * LANES : (t + 1) * LANES] = part.astype(BF)


def owned_kernel(got_ref, out_ref, wide):
    owners, chans, cap = got_ref.shape
    pitch = owners + 1
    for h in range(cap // LANES):
        part = slice(h * LANES, (h + 1) * LANES)
        for s in range(owners):
            wide[h, pl.ds(s, chans, stride=pitch), :] = got_ref[s, :, part].astype(F32)
        for c in range(chans):
            out_ref[c, :, part] = wide[h, c * pitch : c * pitch + owners, :].astype(BF)


def shift(block, axis, step, periodic):
    count = lax.axis_size(axis)
    pairs = [(i, (i + step) % count) for i in range(count) if periodic or 0 <= i + step < count]
    return lax.ppermute(block, axis, pairs)


def body(
    state, forcing, conv_weight, w_first, b_first, w_second, b_second, w_third, b_third,
    w_final, b_final, active, owner, slot, source,
):
    chans, rows, cols = state.shape
    slots = source.size
    cells = rows * cols
    hid = w_second.shape[0]
    owners = lax.axis_size("lon")
    cap = slots // owners
    wide = cols + LANES
    src = source.reshape(1, slots)
    vmem = pl.BlockSpec(memory_space=pltpu.VMEM)
    smem = pl.BlockSpec(memory_space=pltpu.SMEM)
    hbm = pl.BlockSpec(memory_space=pltpu.HBM)

    tile = (chans, rows, LANES)
    pay = pl.pallas_call(
        edges_kernel,
        grid=(1,),
        out_shape=jax.ShapeDtypeStruct((rows, LANES), BF),
        in_specs=[
            pl.BlockSpec(tile, lambda i: (0, 0, 0)),
            pl.BlockSpec(tile, lambda i: (0, 0, cols // LANES - 1)),
        ],
        out_specs=pl.BlockSpec((rows, LANES), lambda i: (0, 0)),
        name="edges",
    )(state, state)
    left = shift(pay, "lon", 1, True)
    right = shift(pay, "lon", -1, True)
    s = state.transpose(1, 0, 2)
    f = forcing.transpose(1, 0, 2)
    taps = conv_weight.reshape(3, 3, chans, chans)
    cw = taps.transpose(1, 2, 0, 3).reshape(3 * chans, 3 * chans)
    whole = pl.BlockSpec((rows, LANES), lambda i: (0, 0))
    up, down = pl.pallas_call(
        rows_kernel,
        grid=(1,),
        out_shape=(jax.ShapeDtypeStruct((chans, wide), BF),) * 2,
        in_specs=[
            whole,
            whole,
            pl.BlockSpec((1, chans, cols), lambda i: (0, 0, 0)),
            pl.BlockSpec((1, chans, cols), lambda i: (rows - 1, 0, 0)),
        ],
        out_specs=(pl.BlockSpec((chans, wide), lambda i: (0, 0)),) * 2,
        name="rows",
    )(left, right, s, s)
    top = shift(down, "lat", 1, False)
    bot = shift(up, "lat", -1, False)

    chunks = rows // CHUNK
    tile_all = (rows, chans, cols)
    dyn, tend, send = pl.pallas_call(
        columns_kernel,
        out_shape=(
            jax.ShapeDtypeStruct(tile_all, BF),
            jax.ShapeDtypeStruct((slots, 2 * chans), BF),
            jax.ShapeDtypeStruct((owners, chans, cap), BF),
        ),
        in_specs=[smem, hbm] + [vmem] * 4 + [hbm, vmem] + [hbm, vmem] * 4 + [vmem],
        out_specs=(hbm,) * 3,
        scratch_shapes=[
            pltpu.VMEM((rows + 2, chans, wide), BF),
            pltpu.VMEM((cells + 8, 2 * chans), F32),
            pltpu.VMEM(tile_all, BF),
            pltpu.VMEM(tile_all, BF),
            pltpu.VMEM((GROUP, 2 * chans), F32),
            pltpu.VMEM((GROUP, 2 * chans), F32),
            pltpu.VMEM((2 * LANES, hid), BF),
            pltpu.VMEM(w_second.shape, BF),
            pltpu.VMEM(w_third.shape, BF),
            pltpu.VMEM(w_first.shape, BF),
            pltpu.VMEM(w_second.shape, BF),
            pltpu.VMEM(w_third.shape, BF),
            pltpu.VMEM(w_final.shape, BF),
            pltpu.VMEM((slots, 2 * chans), BF),
            pltpu.VMEM((owners, chans, cap), BF),
            pltpu.SemaphoreType.DMA((chunks,)),
            pltpu.SemaphoreType.DMA((chunks,)),
            pltpu.SemaphoreType.DMA((chunks,)),
            pltpu.SemaphoreType.DMA((4,)),
            pltpu.SemaphoreType.DMA((slots // GROUP // 2,)),
            pltpu.SemaphoreType.DMA((slots // GROUP // 2,)),
        ],
        compiler_params=pltpu.CompilerParams(vmem_limit_bytes=60 << 20),
        cost_estimate=pl.CostEstimate(flops=10_000_000_000, bytes_accessed=8_000_000, transcendentals=12_000_000),
        name="columns",
    )(
        src, s, left, right, top, bot, f, cw, w_first, b_first.reshape(1, hid), w_second,
        b_second.reshape(1, hid), w_third, b_third.reshape(1, hid), w_final,
        b_final.reshape(1, 2 * chans), src,
    )
    got = lax.all_to_all(send, "lon", split_axis=0, concat_axis=0, tiled=True)
    new_state = pl.pallas_call(
        place_kernel,
        out_shape=jax.ShapeDtypeStruct((chans, rows, cols), BF),
        in_specs=[smem, hbm, hbm],
        out_specs=vmem,
        scratch_shapes=[
            pltpu.VMEM((cells + 8, 2 * chans), F32),
            pltpu.VMEM((LANES, 2 * chans), F32),
            pltpu.VMEM(tile_all, BF),
            pltpu.VMEM((slots, 2 * chans), BF),
            pltpu.VMEM((cols // LANES, chans * PITCH, LANES), F32),
            pltpu.SemaphoreType.DMA((2,)),
        ],
        compiler_params=pltpu.CompilerParams(vmem_limit_bytes=60 << 20),
        cost_estimate=pl.CostEstimate(flops=5_000_000_000, bytes_accessed=8_000_000, transcendentals=0),
        name="place",
    )(src, dyn, tend)
    owned = pl.pallas_call(
        owned_kernel,
        out_shape=jax.ShapeDtypeStruct((chans, owners, cap), BF),
        in_specs=[vmem],
        out_specs=vmem,
        scratch_shapes=[pltpu.VMEM((cap // LANES, chans * (owners + 1), LANES), F32)],
        compiler_params=pltpu.CompilerParams(vmem_limit_bytes=16 << 20),
        name="owned",
    )(got)
    return (new_state, owned.reshape(chans, 1, 1, owners, cap))


def solution(mesh):
    field = P(None, "lat", "lon")
    return jax.shard_map(
        body,
        mesh=mesh,
        in_specs=(field, field) + (P(),) * 9 + (P("lat", "lon"),) * 3 + (P("lat", "lon", None),),
        out_specs=(field, P(None, "lat", "lon", None, None)),
        check_vma=False,
    )
```

```python
import jax
import jax.numpy as jnp
from jax import lax
from jax.experimental import pallas as pl
from jax.experimental.pallas import tpu as pltpu
from jax.sharding import PartitionSpec as P

K0 = 0.7978845608028654
K1 = K0 * 0.044715
LANES = 128
GROUP = 512
CHUNK = 8
PITCH = 33
BF = jnp.bfloat16
F32 = jnp.float32


def lane_index(rows):
    return lax.broadcasted_iota(jnp.int32, (rows, LANES), 1)


def half_gelu(y):
    t = jnp.tanh(y * (2.0 * K0 + (8.0 * K1) * (y * y)))
    return (y + y * t).astype(BF)


def edges_kernel(low_ref, high_ref, pay_ref):
    chans, rows, _ = low_ref.shape
    lane = lane_index(rows)
    acc = jnp.zeros((rows, LANES), F32)
    for c in range(chans):
        low = jnp.broadcast_to(low_ref[c].astype(F32)[:, :1], (rows, LANES))
        high = jnp.broadcast_to(high_ref[c].astype(F32)[:, LANES - 1 :], (rows, LANES))
        acc = jnp.where(lane == c, low, jnp.where(lane == chans + c, high, acc))
    pay_ref[...] = acc.astype(BF)


def halo_columns(left_ref, right_ref, chans):
    rows = left_ref.shape[0]
    pad = jnp.zeros((LANES - rows, LANES), F32)
    left = jnp.concatenate([left_ref[...].astype(F32), pad], axis=0).T[chans : 2 * chans]
    right = jnp.concatenate([right_ref[...].astype(F32), pad], axis=0).T[:chans]
    return left, right


def halo_tile(left, right, y, chans):
    lane = lane_index(chans)
    low = jnp.broadcast_to(right[:, y : y + 1], (chans, LANES))
    high = jnp.broadcast_to(left[:, y : y + 1], (chans, LANES))
    return jnp.where(lane == 0, low, jnp.where(lane == LANES - 1, high, 0.0)).astype(BF)


def rows_kernel(left_ref, right_ref, first_ref, last_ref, up_ref, down_ref):
    _, chans, cols = first_ref.shape
    rows = left_ref.shape[0]
    left, right = halo_columns(left_ref, right_ref, chans)
    up_ref[:, :cols] = first_ref[0]
    up_ref[:, cols:] = halo_tile(left, right, 0, chans)
    down_ref[:, :cols] = last_ref[0]
    down_ref[:, cols:] = halo_tile(left, right, rows - 1, chans)


def columns_kernel(
    src_any, s_any, left_any, right_any, top_any, bot_any, f_any, cw_any,
    w1_any, b1_any, w2_any, b2_any, w3_any, b3_any, w4_any, b4_any,
    dyn_any, tend_ref, send_ref,
    src, vsrc_ref, left_ref, right_ref, cw_ref, ext, feats, f_ref, dyn_ref, buf0, buf1, w1h, w2h, w3h,
    w1_ref, w2_ref, w3_ref, w4_ref, b1_ref, b2_ref, b3_ref, b4_ref,
    tend_buf, send_buf, s_sems, f_sems, dyn_sems, first_sems, w_sems, tend_sems, send_sems,
):
    rows, chans, cols = f_ref.shape
    cells = rows * cols
    owners, _, cap = send_ref.shape
    slots = tend_ref.shape[0]
    groups = slots // GROUP
    wide = cols + LANES
    chunks = rows // CHUNK

    def s_load(k):
        at = k * CHUNK
        target = ext.at[pl.ds(at + 1, CHUNK), :, pl.ds(0, cols)]
        return pltpu.make_async_copy(s_any.at[pl.ds(at, CHUNK)], target, s_sems.at[k])

    def f_load(k):
        part = pl.ds(k * CHUNK, CHUNK)
        return pltpu.make_async_copy(f_any.at[part], f_ref.at[part], f_sems.at[k])

    def dyn_store(k):
        part = pl.ds(k * CHUNK, CHUNK)
        return pltpu.make_async_copy(dyn_ref.at[part], dyn_any.at[part], dyn_sems.at[k])

    firsts = [
        pltpu.make_async_copy(source, target, first_sems.at[k])
        for k, (source, target) in enumerate(
            (
                (left_any, left_ref),
                (right_any, right_ref),
                (cw_any, cw_ref),
                (top_any, ext.at[0]),
                (bot_any, ext.at[rows + 1]),
            )
        )
    ]
    loads = [
        pltpu.make_async_copy(source, target, w_sems.at[k])
        for k, (source, target) in enumerate(
            (
                (src_any, src),
                (src_any, vsrc_ref),
                (w1_any, w1_ref),
                (b1_any, b1_ref),
                (w2_any, w2_ref),
                (b2_any, b2_ref),
                (w3_any, w3_ref),
                (b3_any, b3_ref),
                (w4_any, w4_ref),
                (b4_any, b4_ref),
            )
        )
    ]
    for load in firsts:
        load.start()
    for k in range(chunks):
        s_load(k).start()
        f_load(k).start()
    for load in loads:
        load.start()
    for load in firsts:
        load.wait()
    left, right = halo_columns(left_ref, right_ref, chans)
    for y in range(rows):
        ext[y + 1, :, cols:] = halo_tile(left, right, y, chans)
    feats[cells : cells + 8, :] = jnp.zeros((8, 2 * chans), F32)

    def conv_row(y):
        x = ext[pl.ds(y, 3)].reshape(3 * chans, wide)
        p = jnp.dot(cw_ref[...], x, preferred_element_type=F32)
        total = (
            x[chans : 2 * chans, :cols].astype(F32)
            + p[chans : 2 * chans, :cols]
            + pltpu.roll(p[:chans], 1, 1)[:, :cols]
            + pltpu.roll(p[2 * chans :], wide - 1, 1)[:, :cols]
        )
        dyn = total.astype(BF)
        dyn_ref[y] = dyn
        both = jnp.concatenate([dyn.astype(F32), f_ref[y].astype(F32)], axis=0)
        feats[pl.ds(pl.multiple_of(y * cols, LANES), cols), :] = both.T

    s_load(0).wait()

    def chunk(k, carry):
        @pl.when(k < chunks - 1)
        def _():
            s_load(jnp.minimum(k + 1, chunks - 1)).wait()

        f_load(k).wait()
        for n in range(CHUNK):
            conv_row(k * CHUNK + n)
        dyn_store(k).start()
        return carry

    lax.fori_loop(0, chunks, chunk, 0)

    for load in loads:
        load.wait()
    hid = w2h.shape[0]
    half = b1_ref[...] * 0.5
    high = half.astype(BF)
    rest = half - high.astype(F32)
    mid = rest.astype(BF)
    low = (rest - mid.astype(F32)).astype(BF)
    row = lax.broadcasted_iota(jnp.int32, (LANES, hid), 0)
    w1h[:LANES] = w1_ref[...] * BF(0.5)
    w1h[LANES:] = jnp.where(
        row == 0, high.astype(F32), jnp.where(row == 1, mid.astype(F32), jnp.where(row == 2, low.astype(F32), 0.0))
    ).astype(BF)
    w2h[...] = w2_ref[...] * BF(0.5)
    w3h[...] = w3_ref[...] * BF(0.5)

    def fetch(g, buf, start, stop):
        base = jnp.minimum(g, groups - 1) * GROUP
        for r in range(start, stop, 8):
            rows8 = feats[pl.ds(src[0, base + r], 8, stride=0), :]
            for k in range(1, 8):
                rows8 = jnp.where(sub == k, feats[pl.ds(src[0, base + r + k], 8, stride=0), :], rows8)
            buf[r : r + 8, :] = rows8

    sub = lax.broadcasted_iota(jnp.int32, (8, LANES), 0)
    ones = jnp.ones((GROUP, LANES), BF)

    each = GROUP // cap

    pairs = groups // 2
    stages = ((0, pairs - 1), (pairs - 1, pairs))

    def outward(n):
        start, stop = stages[n]
        rows_part = pl.ds(start * 2 * GROUP, (stop - start) * 2 * GROUP)
        owner_part = pl.ds(start * 2 * each, (stop - start) * 2 * each)
        return (
            pltpu.make_async_copy(tend_buf.at[rows_part], tend_ref.at[rows_part], tend_sems.at[n]),
            pltpu.make_async_copy(send_buf.at[owner_part], send_ref.at[owner_part], send_sems.at[n]),
        )

    def net(g, buf, following):
        part = GROUP // 4
        h = jnp.concatenate([buf[...].astype(BF), ones], axis=1)
        fetch(g + 1, following, 0, part)
        h = half_gelu(jnp.dot(h, w1h[...], preferred_element_type=F32))
        fetch(g + 1, following, part, 2 * part)
        h = half_gelu(jnp.dot(h, w2h[...], preferred_element_type=F32) + b2_ref[...] * 0.5)
        fetch(g + 1, following, 2 * part, 3 * part)
        h = half_gelu(jnp.dot(h, w3h[...], preferred_element_type=F32) + b3_ref[...] * 0.5)
        fetch(g + 1, following, 3 * part, GROUP)
        out = jnp.dot(h, w4_ref[...], preferred_element_type=F32) + b4_ref[...]
        flip = out.T[chans:]
        tend_buf[pl.ds(pl.multiple_of(g * GROUP, GROUP), GROUP), :] = out.astype(BF)
        for j in range(each):
            at = pl.multiple_of((g * each + j) * cap, LANES)
            filled = vsrc_ref[:, pl.ds(at, cap)] < cells
            diag = jnp.where(filled, flip[:, j * cap : (j + 1) * cap], 0.0)
            send_buf[g * each + j] = diag.astype(BF)

    fetch(0, buf0, 0, GROUP)

    def pair(i, carry):
        net(2 * i, buf0, buf1)
        net(2 * i + 1, buf1, buf0)
        return carry

    for n, (start, stop) in enumerate(stages):
        lax.fori_loop(start, stop, pair, 0)
        for copy in outward(n):
            copy.start()
    for n in range(len(stages)):
        for copy in outward(n):
            copy.wait()
    for k in range(chunks):
        dyn_store(k).wait()


def place_kernel(src, dyn_any, tend_any, new_ref, acc, rows_f32, dyn_ref, tend_ref, new_wide, sems):
    chans, rows, cols = new_ref.shape
    slots = tend_ref.shape[0]
    tend_copy = pltpu.make_async_copy(tend_any, tend_ref, sems.at[0])
    tend_copy.start()
    dyn_copy = pltpu.make_async_copy(dyn_any, dyn_ref, sems.at[1])
    dyn_copy.start()
    acc[...] = jnp.zeros(acc.shape, F32)
    tend_copy.wait()

    def block(n, carry):
        base = n * LANES
        rows_f32[...] = tend_ref[pl.ds(pl.multiple_of(base, LANES), LANES), :].astype(F32)
        for r in range(LANES):
            acc[pl.ds(src[0, base + r], 1), :] = rows_f32[pl.ds(r, 1), :]
        return carry

    lax.fori_loop(0, slots // LANES, block, 0)
    dyn_copy.wait()

    def row(y, carry):
        part = acc[pl.ds(pl.multiple_of(y * cols, LANES), cols), :].T[:chans]
        total = dyn_ref[y].astype(F32) + part
        for t in range(cols // LANES):
            new_wide[t, pl.ds(y, chans, stride=PITCH), :] = total[:, t * LANES : (t + 1) * LANES]
        return carry

    lax.fori_loop(0, rows, row, 0, unroll=4)
    for c in range(chans):
        for t in range(cols // LANES):
            part = new_wide[t, c * PITCH : c * PITCH + rows, :]
            new_ref[c, :, t * LANES : (t + 1) * LANES] = part.astype(BF)


def owned_kernel(got_ref, out_ref, wide):
    owners, chans, cap = got_ref.shape
    pitch = owners + 1
    for h in range(cap // LANES):
        part = slice(h * LANES, (h + 1) * LANES)
        for s in range(owners):
            wide[h, pl.ds(s, chans, stride=pitch), :] = got_ref[s, :, part].astype(F32)
        for c in range(chans):
            out_ref[c, :, part] = wide[h, c * pitch : c * pitch + owners, :].astype(BF)


def shift(block, axis, step, periodic):
    count = lax.axis_size(axis)
    pairs = [(i, (i + step) % count) for i in range(count) if periodic or 0 <= i + step < count]
    return lax.ppermute(block, axis, pairs)


def body(
    state, forcing, conv_weight, w_first, b_first, w_second, b_second, w_third, b_third,
    w_final, b_final, active, owner, slot, source,
):
    chans, rows, cols = state.shape
    slots = source.size
    cells = rows * cols
    hid = w_second.shape[0]
    owners = lax.axis_size("lon")
    cap = slots // owners
    wide = cols + LANES
    src = source.reshape(1, slots)
    vmem = pl.BlockSpec(memory_space=pltpu.VMEM)
    smem = pl.BlockSpec(memory_space=pltpu.SMEM)
    hbm = pl.BlockSpec(memory_space=pltpu.HBM)

    tile = (chans, rows, LANES)
    pay = pl.pallas_call(
        edges_kernel,
        grid=(1,),
        out_shape=jax.ShapeDtypeStruct((rows, LANES), BF),
        in_specs=[
            pl.BlockSpec(tile, lambda i: (0, 0, 0)),
            pl.BlockSpec(tile, lambda i: (0, 0, cols // LANES - 1)),
        ],
        out_specs=pl.BlockSpec((rows, LANES), lambda i: (0, 0)),
        compiler_params=pltpu.CompilerParams(vmem_limit_bytes=8 << 20),
        name="edges",
    )(state, state)
    left = shift(pay, "lon", 1, True)
    right = shift(pay, "lon", -1, True)
    s = state.transpose(1, 0, 2)
    f = forcing.transpose(1, 0, 2)
    taps = conv_weight.reshape(3, 3, chans, chans)
    cw = taps.transpose(1, 2, 0, 3).reshape(3 * chans, 3 * chans)
    whole = pl.BlockSpec((rows, LANES), lambda i: (0, 0))
    up, down = pl.pallas_call(
        rows_kernel,
        grid=(1,),
        out_shape=(jax.ShapeDtypeStruct((chans, wide), BF),) * 2,
        in_specs=[
            whole,
            whole,
            pl.BlockSpec((1, chans, cols), lambda i: (0, 0, 0)),
            pl.BlockSpec((1, chans, cols), lambda i: (rows - 1, 0, 0)),
        ],
        out_specs=(pl.BlockSpec((chans, wide), lambda i: (0, 0)),) * 2,
        compiler_params=pltpu.CompilerParams(vmem_limit_bytes=4 << 20),
        name="rows",
    )(left, right, s, s)
    top = shift(down, "lat", 1, False)
    bot = shift(up, "lat", -1, False)

    chunks = rows // CHUNK
    tile_all = (rows, chans, cols)
    dyn, tend, send = pl.pallas_call(
        columns_kernel,
        out_shape=(
            jax.ShapeDtypeStruct(tile_all, BF),
            jax.ShapeDtypeStruct((slots, 2 * chans), BF),
            jax.ShapeDtypeStruct((owners, chans, cap), BF),
        ),
        in_specs=[hbm] * 16,
        out_specs=(hbm,) * 3,
        scratch_shapes=[
            pltpu.SMEM((1, slots), jnp.int32),
            pltpu.VMEM((1, slots), jnp.int32),
            pltpu.VMEM((rows, LANES), BF),
            pltpu.VMEM((rows, LANES), BF),
            pltpu.VMEM(cw.shape, BF),
            pltpu.VMEM((rows + 2, chans, wide), BF),
            pltpu.VMEM((cells + 8, 2 * chans), F32),
            pltpu.VMEM(tile_all, BF),
            pltpu.VMEM(tile_all, BF),
            pltpu.VMEM((GROUP, 2 * chans), F32),
            pltpu.VMEM((GROUP, 2 * chans), F32),
            pltpu.VMEM((2 * LANES, hid), BF),
            pltpu.VMEM(w_second.shape, BF),
            pltpu.VMEM(w_third.shape, BF),
            pltpu.VMEM(w_first.shape, BF),
            pltpu.VMEM(w_second.shape, BF),
            pltpu.VMEM(w_third.shape, BF),
            pltpu.VMEM(w_final.shape, BF),
            pltpu.VMEM((1, hid), F32),
            pltpu.VMEM((1, hid), F32),
            pltpu.VMEM((1, hid), F32),
            pltpu.VMEM((1, 2 * chans), F32),
            pltpu.VMEM((slots, 2 * chans), BF),
            pltpu.VMEM((owners, chans, cap), BF),
            pltpu.SemaphoreType.DMA((chunks,)),
            pltpu.SemaphoreType.DMA((chunks,)),
            pltpu.SemaphoreType.DMA((chunks,)),
            pltpu.SemaphoreType.DMA((5,)),
            pltpu.SemaphoreType.DMA((10,)),
            pltpu.SemaphoreType.DMA((2,)),
            pltpu.SemaphoreType.DMA((2,)),
        ],
        compiler_params=pltpu.CompilerParams(vmem_limit_bytes=60 << 20),
        cost_estimate=pl.CostEstimate(flops=10_000_000_000, bytes_accessed=8_000_000, transcendentals=12_000_000),
        name="columns",
    )(
        src, s, left, right, top, bot, f, cw, w_first, b_first.reshape(1, hid), w_second,
        b_second.reshape(1, hid), w_third, b_third.reshape(1, hid), w_final,
        b_final.reshape(1, 2 * chans),
    )
    got = lax.all_to_all(send, "lon", split_axis=0, concat_axis=0, tiled=True)
    new_state = pl.pallas_call(
        place_kernel,
        out_shape=jax.ShapeDtypeStruct((chans, rows, cols), BF),
        in_specs=[smem, hbm, hbm],
        out_specs=vmem,
        scratch_shapes=[
            pltpu.VMEM((cells + 8, 2 * chans), F32),
            pltpu.VMEM((LANES, 2 * chans), F32),
            pltpu.VMEM(tile_all, BF),
            pltpu.VMEM((slots, 2 * chans), BF),
            pltpu.VMEM((cols // LANES, chans * PITCH, LANES), F32),
            pltpu.SemaphoreType.DMA((2,)),
        ],
        compiler_params=pltpu.CompilerParams(vmem_limit_bytes=60 << 20),
        cost_estimate=pl.CostEstimate(flops=5_000_000_000, bytes_accessed=8_000_000, transcendentals=0),
        name="place",
    )(src, dyn, tend)
    owned = pl.pallas_call(
        owned_kernel,
        out_shape=jax.ShapeDtypeStruct((chans, owners, cap), BF),
        in_specs=[vmem],
        out_specs=vmem,
        scratch_shapes=[pltpu.VMEM((cap // LANES, chans * (owners + 1), LANES), F32)],
        compiler_params=pltpu.CompilerParams(vmem_limit_bytes=16 << 20),
        name="owned",
    )(got)
    return (new_state, owned.reshape(chans, 1, 1, owners, cap))


def solution(mesh):
    field = P(None, "lat", "lon")
    return jax.shard_map(
        body,
        mesh=mesh,
        in_specs=(field, field) + (P(),) * 9 + (P("lat", "lon"),) * 3 + (P("lat", "lon", None),),
        out_specs=(field, P(None, "lat", "lon", None, None)),
        check_vma=False,
    )
```

```python
import jax
import jax.numpy as jnp
from jax import lax
from jax.experimental import pallas as pl
from jax.experimental.pallas import tpu as pltpu
from jax.sharding import PartitionSpec as P

K0 = 0.7978845608028654
K1 = K0 * 0.044715
LANES = 128
GROUP = 512
CHUNK = 8
PITCH = 33
BF = jnp.bfloat16
F32 = jnp.float32


def lane_index(rows):
    return lax.broadcasted_iota(jnp.int32, (rows, LANES), 1)


def half_gelu(y):
    t = jnp.tanh(y * (2.0 * K0 + (8.0 * K1) * (y * y)))
    return (y + y * t).astype(BF)


def edges_kernel(low_ref, high_ref, pay_ref):
    chans, rows, _ = low_ref.shape
    lane = lane_index(rows)
    acc = jnp.zeros((rows, LANES), F32)
    for c in range(chans):
        low = jnp.broadcast_to(low_ref[c].astype(F32)[:, :1], (rows, LANES))
        high = jnp.broadcast_to(high_ref[c].astype(F32)[:, LANES - 1 :], (rows, LANES))
        acc = jnp.where(lane == c, low, jnp.where(lane == chans + c, high, acc))
    pay_ref[...] = acc.astype(BF)


def halo_columns(left_ref, right_ref, chans):
    rows = left_ref.shape[0]
    pad = jnp.zeros((LANES - rows, LANES), F32)
    left = jnp.concatenate([left_ref[...].astype(F32), pad], axis=0).T[chans : 2 * chans]
    right = jnp.concatenate([right_ref[...].astype(F32), pad], axis=0).T[:chans]
    return left, right


def halo_tile(left, right, y, chans):
    lane = lane_index(chans)
    low = jnp.broadcast_to(right[:, y : y + 1], (chans, LANES))
    high = jnp.broadcast_to(left[:, y : y + 1], (chans, LANES))
    return jnp.where(lane == 0, low, jnp.where(lane == LANES - 1, high, 0.0)).astype(BF)


def rows_kernel(left_ref, right_ref, first_ref, last_ref, up_ref, down_ref):
    _, chans, cols = first_ref.shape
    rows = left_ref.shape[0]
    left, right = halo_columns(left_ref, right_ref, chans)
    up_ref[:, :cols] = first_ref[0]
    up_ref[:, cols:] = halo_tile(left, right, 0, chans)
    down_ref[:, :cols] = last_ref[0]
    down_ref[:, cols:] = halo_tile(left, right, rows - 1, chans)


def columns_kernel(
    src_any, s_any, left_any, right_any, top_any, bot_any, f_any, cw_any,
    w1_any, b1_any, w2_any, b2_any, w3_any, b3_any, w4_any, b4_any,
    dyn_any, tend_ref, send_ref,
    src, vsrc_ref, left_ref, right_ref, cw_ref, ext, feats, f_ref, dyn_ref, buf0, buf1, w1h, w2h, w3h,
    w1_ref, w2_ref, w3_ref, w4_ref, b1_ref, b2_ref, b3_ref, b4_ref,
    tend_buf, send_buf, table, s_sems, f_sems, dyn_sems, first_sems, w_sems, tend_sems, send_sems,
):
    rows, chans, cols = f_ref.shape
    cells = rows * cols
    owners, _, cap = send_ref.shape
    slots = tend_ref.shape[0]
    wide = cols + LANES
    chunks = rows // CHUNK

    def s_load(k):
        at = k * CHUNK
        target = ext.at[pl.ds(at + 1, CHUNK), :, pl.ds(0, cols)]
        return pltpu.make_async_copy(s_any.at[pl.ds(at, CHUNK)], target, s_sems.at[k])

    def f_load(k):
        part = pl.ds(k * CHUNK, CHUNK)
        return pltpu.make_async_copy(f_any.at[part], f_ref.at[part], f_sems.at[k])

    def dyn_store(k):
        part = pl.ds(k * CHUNK, CHUNK)
        return pltpu.make_async_copy(dyn_ref.at[part], dyn_any.at[part], dyn_sems.at[k])

    firsts = [
        pltpu.make_async_copy(source, target, first_sems.at[k])
        for k, (source, target) in enumerate(
            (
                (left_any, left_ref),
                (right_any, right_ref),
                (cw_any, cw_ref),
                (top_any, ext.at[0]),
                (bot_any, ext.at[rows + 1]),
            )
        )
    ]
    loads = [
        pltpu.make_async_copy(source, target, w_sems.at[k])
        for k, (source, target) in enumerate(
            (
                (src_any, src),
                (src_any, vsrc_ref),
                (w1_any, w1_ref),
                (b1_any, b1_ref),
                (w2_any, w2_ref),
                (b2_any, b2_ref),
                (w3_any, w3_ref),
                (b3_any, b3_ref),
                (w4_any, w4_ref),
                (b4_any, b4_ref),
            )
        )
    ]
    for load in firsts:
        load.start()
    for k in range(chunks):
        s_load(k).start()
        f_load(k).start()
    for load in loads:
        load.start()
    send_buf[...] = jnp.zeros(send_buf.shape, BF)
    for load in firsts:
        load.wait()
    left, right = halo_columns(left_ref, right_ref, chans)
    for y in range(rows):
        ext[y + 1, :, cols:] = halo_tile(left, right, y, chans)
    feats[cells : cells + 8, :] = jnp.zeros((8, 2 * chans), F32)

    def conv_row(y):
        x = ext[pl.ds(y, 3)].reshape(3 * chans, wide)
        p = jnp.dot(cw_ref[...], x, preferred_element_type=F32)
        total = (
            x[chans : 2 * chans, :cols].astype(F32)
            + p[chans : 2 * chans, :cols]
            + pltpu.roll(p[:chans], 1, 1)[:, :cols]
            + pltpu.roll(p[2 * chans :], wide - 1, 1)[:, :cols]
        )
        dyn = total.astype(BF)
        dyn_ref[y] = dyn
        both = jnp.concatenate([dyn.astype(F32), f_ref[y].astype(F32)], axis=0)
        feats[pl.ds(pl.multiple_of(y * cols, LANES), cols), :] = both.T

    s_load(0).wait()

    def chunk(k, carry):
        @pl.when(k < chunks - 1)
        def _():
            s_load(jnp.minimum(k + 1, chunks - 1)).wait()

        f_load(k).wait()
        for n in range(CHUNK):
            conv_row(k * CHUNK + n)
        dyn_store(k).start()
        return carry

    lax.fori_loop(0, chunks, chunk, 0)

    for load in loads:
        load.wait()
    hid = w2h.shape[0]
    half = b1_ref[...] * 0.5
    high = half.astype(BF)
    rest = half - high.astype(F32)
    mid = rest.astype(BF)
    low = (rest - mid.astype(F32)).astype(BF)
    row = lax.broadcasted_iota(jnp.int32, (LANES, hid), 0)
    w1h[:LANES] = w1_ref[...] * BF(0.5)
    w1h[LANES:] = jnp.where(
        row == 0, high.astype(F32), jnp.where(row == 1, mid.astype(F32), jnp.where(row == 2, low.astype(F32), 0.0))
    ).astype(BF)
    w2h[...] = w2_ref[...] * BF(0.5)
    w3h[...] = w3_ref[...] * BF(0.5)

    each = GROUP // cap
    step = 2 * each
    split = owners - step

    def list_owners(first, stop, begin):
        def scan(o, n):
            table[n] = o
            return n + (src[0, o * cap] < cells).astype(jnp.int32)

        end = lax.fori_loop(first, stop, scan, begin)
        last = table[jnp.maximum(end - 1, 0)]
        for extra in range(step):
            table[end + extra] = last
        return begin + (end - begin + step - 1) // step * step

    middle = list_owners(0, split, jnp.int32(0))
    finish = list_owners(split, owners, middle)

    def fetch(g, buf, start, stop):
        entry = jnp.minimum(g * each, jnp.maximum(finish - each, 0))
        for r in range(start, stop, 8):
            base = table[entry + r // cap] * cap + r % cap
            rows8 = feats[pl.ds(src[0, base], 8, stride=0), :]
            for k in range(1, 8):
                rows8 = jnp.where(sub == k, feats[pl.ds(src[0, base + k], 8, stride=0), :], rows8)
            buf[r : r + 8, :] = rows8

    sub = lax.broadcasted_iota(jnp.int32, (8, LANES), 0)
    ones = jnp.ones((GROUP, LANES), BF)

    stages = ((0, split, 0, middle // step), (split, owners, middle // step, finish // step))

    def outward(n):
        start, stop = stages[n][:2]
        rows_part = pl.ds(start * cap, (stop - start) * cap)
        owner_part = pl.ds(start, stop - start)
        return (
            pltpu.make_async_copy(tend_buf.at[rows_part], tend_ref.at[rows_part], tend_sems.at[n]),
            pltpu.make_async_copy(send_buf.at[owner_part], send_ref.at[owner_part], send_sems.at[n]),
        )

    def net(g, buf, following):
        part = GROUP // 4
        h = jnp.concatenate([buf[...].astype(BF), ones], axis=1)
        fetch(g + 1, following, 0, part)
        h = half_gelu(jnp.dot(h, w1h[...], preferred_element_type=F32))
        fetch(g + 1, following, part, 2 * part)
        h = half_gelu(jnp.dot(h, w2h[...], preferred_element_type=F32) + b2_ref[...] * 0.5)
        fetch(g + 1, following, 2 * part, 3 * part)
        h = half_gelu(jnp.dot(h, w3h[...], preferred_element_type=F32) + b3_ref[...] * 0.5)
        fetch(g + 1, following, 3 * part, GROUP)
        out = jnp.dot(h, w4_ref[...], preferred_element_type=F32) + b4_ref[...]
        flip = out.T[chans:]
        for j in range(each):
            o = table[g * each + j]
            rows_part = pl.ds(pl.multiple_of(o * cap, LANES), cap)
            tend_buf[rows_part, :] = out[j * cap : (j + 1) * cap].astype(BF)
            filled = vsrc_ref[:, rows_part] < cells
            send_buf[o] = jnp.where(filled, flip[:, j * cap : (j + 1) * cap], 0.0).astype(BF)

    fetch(0, buf0, 0, GROUP)

    def pair(i, carry):
        net(2 * i, buf0, buf1)
        net(2 * i + 1, buf1, buf0)
        return carry

    for n, (_, _, start, stop) in enumerate(stages):
        lax.fori_loop(start, stop, pair, 0)
        for copy in outward(n):
            copy.start()
    for n in range(len(stages)):
        for copy in outward(n):
            copy.wait()
    for k in range(chunks):
        dyn_store(k).wait()


def place_kernel(src, dyn_any, tend_any, new_ref, acc, rows_f32, dyn_ref, tend_ref, new_wide, sems):
    chans, rows, cols = new_ref.shape
    slots = tend_ref.shape[0]
    tend_copy = pltpu.make_async_copy(tend_any, tend_ref, sems.at[0])
    tend_copy.start()
    dyn_copy = pltpu.make_async_copy(dyn_any, dyn_ref, sems.at[1])
    dyn_copy.start()
    acc[...] = jnp.zeros(acc.shape, F32)
    tend_copy.wait()

    def block(n, carry):
        base = n * LANES
        rows_f32[...] = tend_ref[pl.ds(pl.multiple_of(base, LANES), LANES), :].astype(F32)
        for r in range(LANES):
            acc[pl.ds(src[0, base + r], 1), :] = rows_f32[pl.ds(r, 1), :]
        return carry

    lax.fori_loop(0, slots // LANES, block, 0)
    dyn_copy.wait()

    def row(y, carry):
        part = acc[pl.ds(pl.multiple_of(y * cols, LANES), cols), :].T[:chans]
        total = dyn_ref[y].astype(F32) + part
        for t in range(cols // LANES):
            new_wide[t, pl.ds(y, chans, stride=PITCH), :] = total[:, t * LANES : (t + 1) * LANES]
        return carry

    lax.fori_loop(0, rows, row, 0, unroll=4)
    for c in range(chans):
        for t in range(cols // LANES):
            part = new_wide[t, c * PITCH : c * PITCH + rows, :]
            new_ref[c, :, t * LANES : (t + 1) * LANES] = part.astype(BF)


def owned_kernel(got_ref, out_ref, wide):
    owners, chans, cap = got_ref.shape
    pitch = owners + 1
    for h in range(cap // LANES):
        part = slice(h * LANES, (h + 1) * LANES)
        for s in range(owners):
            wide[h, pl.ds(s, chans, stride=pitch), :] = got_ref[s, :, part].astype(F32)
        for c in range(chans):
            out_ref[c, :, part] = wide[h, c * pitch : c * pitch + owners, :].astype(BF)


def shift(block, axis, step, periodic):
    count = lax.axis_size(axis)
    pairs = [(i, (i + step) % count) for i in range(count) if periodic or 0 <= i + step < count]
    return lax.ppermute(block, axis, pairs)


def body(
    state, forcing, conv_weight, w_first, b_first, w_second, b_second, w_third, b_third,
    w_final, b_final, active, owner, slot, source,
):
    chans, rows, cols = state.shape
    slots = source.size
    cells = rows * cols
    hid = w_second.shape[0]
    owners = lax.axis_size("lon")
    cap = slots // owners
    wide = cols + LANES
    src = source.reshape(1, slots)
    vmem = pl.BlockSpec(memory_space=pltpu.VMEM)
    smem = pl.BlockSpec(memory_space=pltpu.SMEM)
    hbm = pl.BlockSpec(memory_space=pltpu.HBM)

    tile = (chans, rows, LANES)
    pay = pl.pallas_call(
        edges_kernel,
        grid=(1,),
        out_shape=jax.ShapeDtypeStruct((rows, LANES), BF),
        in_specs=[
            pl.BlockSpec(tile, lambda i: (0, 0, 0)),
            pl.BlockSpec(tile, lambda i: (0, 0, cols // LANES - 1)),
        ],
        out_specs=pl.BlockSpec((rows, LANES), lambda i: (0, 0)),
        compiler_params=pltpu.CompilerParams(vmem_limit_bytes=8 << 20),
        name="edges",
    )(state, state)
    left = shift(pay, "lon", 1, True)
    right = shift(pay, "lon", -1, True)
    s = state.transpose(1, 0, 2)
    f = forcing.transpose(1, 0, 2)
    taps = conv_weight.reshape(3, 3, chans, chans)
    cw = taps.transpose(1, 2, 0, 3).reshape(3 * chans, 3 * chans)
    whole = pl.BlockSpec((rows, LANES), lambda i: (0, 0))
    up, down = pl.pallas_call(
        rows_kernel,
        grid=(1,),
        out_shape=(jax.ShapeDtypeStruct((chans, wide), BF),) * 2,
        in_specs=[
            whole,
            whole,
            pl.BlockSpec((1, chans, cols), lambda i: (0, 0, 0)),
            pl.BlockSpec((1, chans, cols), lambda i: (rows - 1, 0, 0)),
        ],
        out_specs=(pl.BlockSpec((chans, wide), lambda i: (0, 0)),) * 2,
        compiler_params=pltpu.CompilerParams(vmem_limit_bytes=4 << 20),
        name="rows",
    )(left, right, s, s)
    top = shift(down, "lat", 1, False)
    bot = shift(up, "lat", -1, False)

    chunks = rows // CHUNK
    tile_all = (rows, chans, cols)
    dyn, tend, send = pl.pallas_call(
        columns_kernel,
        out_shape=(
            jax.ShapeDtypeStruct(tile_all, BF),
            jax.ShapeDtypeStruct((slots, 2 * chans), BF),
            jax.ShapeDtypeStruct((owners, chans, cap), BF),
        ),
        in_specs=[hbm] * 16,
        out_specs=(hbm,) * 3,
        scratch_shapes=[
            pltpu.SMEM((1, slots), jnp.int32),
            pltpu.VMEM((1, slots), jnp.int32),
            pltpu.VMEM((rows, LANES), BF),
            pltpu.VMEM((rows, LANES), BF),
            pltpu.VMEM(cw.shape, BF),
            pltpu.VMEM((rows + 2, chans, wide), BF),
            pltpu.VMEM((cells + 8, 2 * chans), F32),
            pltpu.VMEM(tile_all, BF),
            pltpu.VMEM(tile_all, BF),
            pltpu.VMEM((GROUP, 2 * chans), F32),
            pltpu.VMEM((GROUP, 2 * chans), F32),
            pltpu.VMEM((2 * LANES, hid), BF),
            pltpu.VMEM(w_second.shape, BF),
            pltpu.VMEM(w_third.shape, BF),
            pltpu.VMEM(w_first.shape, BF),
            pltpu.VMEM(w_second.shape, BF),
            pltpu.VMEM(w_third.shape, BF),
            pltpu.VMEM(w_final.shape, BF),
            pltpu.VMEM((1, hid), F32),
            pltpu.VMEM((1, hid), F32),
            pltpu.VMEM((1, hid), F32),
            pltpu.VMEM((1, 2 * chans), F32),
            pltpu.VMEM((slots, 2 * chans), BF),
            pltpu.VMEM((owners, chans, cap), BF),
            pltpu.SMEM((2 * owners,), jnp.int32),
            pltpu.SemaphoreType.DMA((chunks,)),
            pltpu.SemaphoreType.DMA((chunks,)),
            pltpu.SemaphoreType.DMA((chunks,)),
            pltpu.SemaphoreType.DMA((5,)),
            pltpu.SemaphoreType.DMA((10,)),
            pltpu.SemaphoreType.DMA((2,)),
            pltpu.SemaphoreType.DMA((2,)),
        ],
        compiler_params=pltpu.CompilerParams(vmem_limit_bytes=60 << 20),
        cost_estimate=pl.CostEstimate(flops=10_000_000_000, bytes_accessed=8_000_000, transcendentals=12_000_000),
        name="columns",
    )(
        src, s, left, right, top, bot, f, cw, w_first, b_first.reshape(1, hid), w_second,
        b_second.reshape(1, hid), w_third, b_third.reshape(1, hid), w_final,
        b_final.reshape(1, 2 * chans),
    )
    got = lax.all_to_all(send, "lon", split_axis=0, concat_axis=0, tiled=True)
    new_state = pl.pallas_call(
        place_kernel,
        out_shape=jax.ShapeDtypeStruct((chans, rows, cols), BF),
        in_specs=[smem, hbm, hbm],
        out_specs=vmem,
        scratch_shapes=[
            pltpu.VMEM((cells + 8, 2 * chans), F32),
            pltpu.VMEM((LANES, 2 * chans), F32),
            pltpu.VMEM(tile_all, BF),
            pltpu.VMEM((slots, 2 * chans), BF),
            pltpu.VMEM((cols // LANES, chans * PITCH, LANES), F32),
            pltpu.SemaphoreType.DMA((2,)),
        ],
        compiler_params=pltpu.CompilerParams(vmem_limit_bytes=60 << 20),
        cost_estimate=pl.CostEstimate(flops=5_000_000_000, bytes_accessed=8_000_000, transcendentals=0),
        name="place",
    )(src, dyn, tend)
    owned = pl.pallas_call(
        owned_kernel,
        out_shape=jax.ShapeDtypeStruct((chans, owners, cap), BF),
        in_specs=[vmem],
        out_specs=vmem,
        scratch_shapes=[pltpu.VMEM((cap // LANES, chans * (owners + 1), LANES), F32)],
        compiler_params=pltpu.CompilerParams(vmem_limit_bytes=16 << 20),
        name="owned",
    )(got)
    return (new_state, owned.reshape(chans, 1, 1, owners, cap))


def solution(mesh):
    field = P(None, "lat", "lon")
    return jax.shard_map(
        body,
        mesh=mesh,
        in_specs=(field, field) + (P(),) * 9 + (P("lat", "lon"),) * 3 + (P("lat", "lon", None),),
        out_specs=(field, P(None, "lat", "lon", None, None)),
        check_vma=False,
    )
```

```python
import jax
import jax.numpy as jnp
from jax import lax
from jax.experimental import pallas as pl
from jax.experimental.pallas import tpu as pltpu
from jax.sharding import PartitionSpec as P

K0 = 0.7978845608028654
K1 = K0 * 0.044715
LANES = 128
GROUP = 512
CHUNK = 16
PITCH = 33
BF = jnp.bfloat16
F32 = jnp.float32


def lane_index(rows):
    return lax.broadcasted_iota(jnp.int32, (rows, LANES), 1)


def half_gelu(y):
    t = jnp.tanh(y * (2.0 * K0 + (8.0 * K1) * (y * y)))
    return (y + y * t).astype(BF)


def edges_kernel(low_ref, high_ref, pay_ref):
    chans, rows, _ = low_ref.shape
    lane = lane_index(rows)
    acc = jnp.zeros((rows, LANES), F32)
    for c in range(chans):
        low = jnp.broadcast_to(low_ref[c].astype(F32)[:, :1], (rows, LANES))
        high = jnp.broadcast_to(high_ref[c].astype(F32)[:, LANES - 1 :], (rows, LANES))
        acc = jnp.where(lane == c, low, jnp.where(lane == chans + c, high, acc))
    pay_ref[...] = acc.astype(BF)


def halo_columns(left_ref, right_ref, chans):
    rows = left_ref.shape[0]
    pad = jnp.zeros((LANES - rows, LANES), F32)
    left = jnp.concatenate([left_ref[...].astype(F32), pad], axis=0).T[chans : 2 * chans]
    right = jnp.concatenate([right_ref[...].astype(F32), pad], axis=0).T[:chans]
    return left, right


def halo_tile(left, right, y, chans):
    lane = lane_index(chans)
    low = jnp.broadcast_to(right[:, y : y + 1], (chans, LANES))
    high = jnp.broadcast_to(left[:, y : y + 1], (chans, LANES))
    return jnp.where(lane == 0, low, jnp.where(lane == LANES - 1, high, 0.0)).astype(BF)


def rows_kernel(left_ref, right_ref, first_ref, last_ref, up_ref, down_ref):
    _, chans, cols = first_ref.shape
    rows = left_ref.shape[0]
    left, right = halo_columns(left_ref, right_ref, chans)
    up_ref[:, :cols] = first_ref[0]
    up_ref[:, cols:] = halo_tile(left, right, 0, chans)
    down_ref[:, :cols] = last_ref[0]
    down_ref[:, cols:] = halo_tile(left, right, rows - 1, chans)


def columns_kernel(
    src_any, s_any, left_any, right_any, top_any, bot_any, f_any, cw_any,
    w1_any, b1_any, w2_any, b2_any, w3_any, b3_any, w4_any, b4_any,
    dyn_any, tend_ref, send_ref,
    src, vsrc_ref, left_ref, right_ref, cw_ref, ext, feats, f_ref, dyn_ref, buf0, buf1, w1h, w2h, w3h,
    w1_ref, w2_ref, w3_ref, w4_ref, b1_ref, b2_ref, b3_ref, b4_ref,
    tend_buf, send_buf, table, s_sems, f_sems, dyn_sems, first_sems, w_sems, tend_sems, send_sems,
):
    rows, chans, cols = f_ref.shape
    cells = rows * cols
    owners, _, cap = send_ref.shape
    slots = tend_ref.shape[0]
    wide = cols + LANES
    chunks = rows // CHUNK

    def s_load(k):
        at = k * CHUNK
        target = ext.at[pl.ds(at + 1, CHUNK), :, pl.ds(0, cols)]
        return pltpu.make_async_copy(s_any.at[pl.ds(at, CHUNK)], target, s_sems.at[k])

    def f_load(k):
        part = pl.ds(k * CHUNK, CHUNK)
        return pltpu.make_async_copy(f_any.at[part], f_ref.at[part], f_sems.at[k])

    def dyn_store(k):
        part = pl.ds(k * CHUNK, CHUNK)
        return pltpu.make_async_copy(dyn_ref.at[part], dyn_any.at[part], dyn_sems.at[k])

    firsts = [
        pltpu.make_async_copy(source, target, first_sems.at[k])
        for k, (source, target) in enumerate(
            (
                (left_any, left_ref),
                (right_any, right_ref),
                (cw_any, cw_ref),
                (top_any, ext.at[0]),
                (bot_any, ext.at[rows + 1]),
            )
        )
    ]
    loads = [
        pltpu.make_async_copy(source, target, w_sems.at[k])
        for k, (source, target) in enumerate(
            (
                (src_any, src),
                (src_any, vsrc_ref),
                (w1_any, w1_ref),
                (b1_any, b1_ref),
                (w2_any, w2_ref),
                (b2_any, b2_ref),
                (w3_any, w3_ref),
                (b3_any, b3_ref),
                (w4_any, w4_ref),
                (b4_any, b4_ref),
            )
        )
    ]
    for load in firsts:
        load.start()
    for k in range(chunks):
        s_load(k).start()
        f_load(k).start()
    for load in loads:
        load.start()
    send_buf[...] = jnp.zeros(send_buf.shape, BF)
    for load in firsts:
        load.wait()
    left, right = halo_columns(left_ref, right_ref, chans)
    for y in range(rows):
        ext[y + 1, :, cols:] = halo_tile(left, right, y, chans)
    feats[cells : cells + 8, :] = jnp.zeros((8, 2 * chans), F32)

    def conv_row(y):
        x = ext[pl.ds(y, 3)].reshape(3 * chans, wide)
        p = jnp.dot(cw_ref[...], x, preferred_element_type=F32)
        total = (
            x[chans : 2 * chans, :cols].astype(F32)
            + p[chans : 2 * chans, :cols]
            + pltpu.roll(p[:chans], 1, 1)[:, :cols]
            + pltpu.roll(p[2 * chans :], wide - 1, 1)[:, :cols]
        )
        dyn = total.astype(BF)
        dyn_ref[y] = dyn
        both = jnp.concatenate([dyn.astype(F32), f_ref[y].astype(F32)], axis=0)
        feats[pl.ds(pl.multiple_of(y * cols, LANES), cols), :] = both.T

    s_load(0).wait()

    def chunk(k, carry):
        @pl.when(k < chunks - 1)
        def _():
            s_load(jnp.minimum(k + 1, chunks - 1)).wait()

        f_load(k).wait()
        for n in range(CHUNK):
            conv_row(k * CHUNK + n)
        dyn_store(k).start()
        return carry

    lax.fori_loop(0, chunks, chunk, 0)

    for load in loads:
        load.wait()
    each = GROUP // cap
    step = 2 * each
    split = owners - step

    def list_owners(first, stop, begin):
        def scan(o, n):
            table[n] = o
            return n + (src[0, o * cap] < cells).astype(jnp.int32)

        end = lax.fori_loop(first, stop, scan, begin)
        last = table[jnp.maximum(end - 1, 0)]
        for extra in range(step):
            table[end + extra] = last
        return begin + (end - begin + step - 1) // step * step

    middle = list_owners(0, split, jnp.int32(0))
    finish = list_owners(split, owners, middle)

    def fetch(g, buf, start, stop):
        entry = jnp.minimum(g * each, jnp.maximum(finish - each, 0))
        for r in range(start, stop, 8):
            base = table[entry + r // cap] * cap + r % cap
            rows8 = feats[pl.ds(src[0, base], 8, stride=0), :]
            for k in range(1, 8):
                rows8 = jnp.where(sub == k, feats[pl.ds(src[0, base + k], 8, stride=0), :], rows8)
            buf[r : r + 8, :] = rows8

    sub = lax.broadcasted_iota(jnp.int32, (8, LANES), 0)
    ones = jnp.ones((GROUP, LANES), BF)

    stages = ((0, split, 0, middle // step), (split, owners, middle // step, finish // step))

    def outward(n):
        start, stop = stages[n][:2]
        rows_part = pl.ds(start * cap, (stop - start) * cap)
        owner_part = pl.ds(start, stop - start)
        return (
            pltpu.make_async_copy(tend_buf.at[rows_part], tend_ref.at[rows_part], tend_sems.at[n]),
            pltpu.make_async_copy(send_buf.at[owner_part], send_ref.at[owner_part], send_sems.at[n]),
        )

    def net(g, buf, following):
        part = GROUP // 4
        h = jnp.concatenate([buf[...].astype(BF), ones], axis=1)
        fetch(g + 1, following, 0, part)
        h = half_gelu(jnp.dot(h, w1h[...], preferred_element_type=F32))
        fetch(g + 1, following, part, 2 * part)
        h = half_gelu(jnp.dot(h, w2h[...], preferred_element_type=F32) + b2_ref[...] * 0.5)
        fetch(g + 1, following, 2 * part, 3 * part)
        h = half_gelu(jnp.dot(h, w3h[...], preferred_element_type=F32) + b3_ref[...] * 0.5)
        fetch(g + 1, following, 3 * part, GROUP)
        out = jnp.dot(h, w4_ref[...], preferred_element_type=F32) + b4_ref[...]
        flip = out.T[chans:]
        for j in range(each):
            o = table[g * each + j]
            rows_part = pl.ds(pl.multiple_of(o * cap, LANES), cap)
            tend_buf[rows_part, :] = out[j * cap : (j + 1) * cap].astype(BF)
            filled = vsrc_ref[:, rows_part] < cells
            send_buf[o] = jnp.where(filled, flip[:, j * cap : (j + 1) * cap], 0.0).astype(BF)

    hid = w2h.shape[0]
    half = b1_ref[...] * 0.5
    high = half.astype(BF)
    rest = half - high.astype(F32)
    mid = rest.astype(BF)
    low = (rest - mid.astype(F32)).astype(BF)
    row = lax.broadcasted_iota(jnp.int32, (LANES, hid), 0)
    w1h[:LANES] = w1_ref[...] * BF(0.5)
    w1h[LANES:] = jnp.where(
        row == 0, high.astype(F32), jnp.where(row == 1, mid.astype(F32), jnp.where(row == 2, low.astype(F32), 0.0))
    ).astype(BF)
    w2h[...] = w2_ref[...] * BF(0.5)
    w3h[...] = w3_ref[...] * BF(0.5)

    fetch(0, buf0, 0, GROUP)

    def pair(i, carry):
        net(2 * i, buf0, buf1)
        net(2 * i + 1, buf1, buf0)
        return carry

    for n, (_, _, start, stop) in enumerate(stages):
        lax.fori_loop(start, stop, pair, 0)
        for copy in outward(n):
            copy.start()
    for n in range(len(stages)):
        for copy in outward(n):
            copy.wait()
    for k in range(chunks):
        dyn_store(k).wait()


def place_kernel(src, dyn_any, tend_any, new_ref, acc, rows_f32, dyn_ref, tend_ref, new_wide, sems):
    chans, rows, cols = new_ref.shape
    slots = tend_ref.shape[0]
    tend_copy = pltpu.make_async_copy(tend_any, tend_ref, sems.at[0])
    tend_copy.start()
    dyn_copy = pltpu.make_async_copy(dyn_any, dyn_ref, sems.at[1])
    dyn_copy.start()
    acc[...] = jnp.zeros(acc.shape, F32)
    tend_copy.wait()

    def block(n, carry):
        base = n * LANES
        rows_f32[...] = tend_ref[pl.ds(pl.multiple_of(base, LANES), LANES), :].astype(F32)
        for r in range(LANES):
            acc[pl.ds(src[0, base + r], 1), :] = rows_f32[pl.ds(r, 1), :]
        return carry

    lax.fori_loop(0, slots // LANES, block, 0)
    dyn_copy.wait()

    def row(y, carry):
        part = acc[pl.ds(pl.multiple_of(y * cols, LANES), cols), :].T[:chans]
        total = dyn_ref[y].astype(F32) + part
        for t in range(cols // LANES):
            new_wide[t, pl.ds(y, chans, stride=PITCH), :] = total[:, t * LANES : (t + 1) * LANES]
        return carry

    lax.fori_loop(0, rows, row, 0, unroll=4)
    for c in range(chans):
        for t in range(cols // LANES):
            part = new_wide[t, c * PITCH : c * PITCH + rows, :]
            new_ref[c, :, t * LANES : (t + 1) * LANES] = part.astype(BF)


def owned_kernel(got_ref, out_ref, wide):
    owners, chans, cap = got_ref.shape
    pitch = owners + 1
    for h in range(cap // LANES):
        part = slice(h * LANES, (h + 1) * LANES)
        for s in range(owners):
            wide[h, pl.ds(s, chans, stride=pitch), :] = got_ref[s, :, part].astype(F32)
        for c in range(chans):
            out_ref[c, :, part] = wide[h, c * pitch : c * pitch + owners, :].astype(BF)


def shift(block, axis, step, periodic):
    count = lax.axis_size(axis)
    pairs = [(i, (i + step) % count) for i in range(count) if periodic or 0 <= i + step < count]
    return lax.ppermute(block, axis, pairs)


def body(
    state, forcing, conv_weight, w_first, b_first, w_second, b_second, w_third, b_third,
    w_final, b_final, active, owner, slot, source,
):
    chans, rows, cols = state.shape
    slots = source.size
    cells = rows * cols
    hid = w_second.shape[0]
    owners = lax.axis_size("lon")
    cap = slots // owners
    wide = cols + LANES
    src = source.reshape(1, slots)
    vmem = pl.BlockSpec(memory_space=pltpu.VMEM)
    smem = pl.BlockSpec(memory_space=pltpu.SMEM)
    hbm = pl.BlockSpec(memory_space=pltpu.HBM)

    tile = (chans, rows, LANES)
    pay = pl.pallas_call(
        edges_kernel,
        grid=(1,),
        out_shape=jax.ShapeDtypeStruct((rows, LANES), BF),
        in_specs=[
            pl.BlockSpec(tile, lambda i: (0, 0, 0)),
            pl.BlockSpec(tile, lambda i: (0, 0, cols // LANES - 1)),
        ],
        out_specs=pl.BlockSpec((rows, LANES), lambda i: (0, 0)),
        compiler_params=pltpu.CompilerParams(vmem_limit_bytes=8 << 20),
        name="edges",
    )(state, state)
    left = shift(pay, "lon", 1, True)
    right = shift(pay, "lon", -1, True)
    s = state.transpose(1, 0, 2)
    f = forcing.transpose(1, 0, 2)
    taps = conv_weight.reshape(3, 3, chans, chans)
    cw = taps.transpose(1, 2, 0, 3).reshape(3 * chans, 3 * chans)
    whole = pl.BlockSpec((rows, LANES), lambda i: (0, 0))
    up, down = pl.pallas_call(
        rows_kernel,
        grid=(1,),
        out_shape=(jax.ShapeDtypeStruct((chans, wide), BF),) * 2,
        in_specs=[
            whole,
            whole,
            pl.BlockSpec((1, chans, cols), lambda i: (0, 0, 0)),
            pl.BlockSpec((1, chans, cols), lambda i: (rows - 1, 0, 0)),
        ],
        out_specs=(pl.BlockSpec((chans, wide), lambda i: (0, 0)),) * 2,
        compiler_params=pltpu.CompilerParams(vmem_limit_bytes=4 << 20),
        name="rows",
    )(left, right, s, s)
    top = shift(down, "lat", 1, False)
    bot = shift(up, "lat", -1, False)

    chunks = rows // CHUNK
    tile_all = (rows, chans, cols)
    dyn, tend, send = pl.pallas_call(
        columns_kernel,
        out_shape=(
            jax.ShapeDtypeStruct(tile_all, BF),
            jax.ShapeDtypeStruct((slots, 2 * chans), BF),
            jax.ShapeDtypeStruct((owners, chans, cap), BF),
        ),
        in_specs=[hbm] * 16,
        out_specs=(hbm,) * 3,
        scratch_shapes=[
            pltpu.SMEM((1, slots), jnp.int32),
            pltpu.VMEM((1, slots), jnp.int32),
            pltpu.VMEM((rows, LANES), BF),
            pltpu.VMEM((rows, LANES), BF),
            pltpu.VMEM(cw.shape, BF),
            pltpu.VMEM((rows + 2, chans, wide), BF),
            pltpu.VMEM((cells + 8, 2 * chans), F32),
            pltpu.VMEM(tile_all, BF),
            pltpu.VMEM(tile_all, BF),
            pltpu.VMEM((GROUP, 2 * chans), F32),
            pltpu.VMEM((GROUP, 2 * chans), F32),
            pltpu.VMEM((2 * LANES, hid), BF),
            pltpu.VMEM(w_second.shape, BF),
            pltpu.VMEM(w_third.shape, BF),
            pltpu.VMEM(w_first.shape, BF),
            pltpu.VMEM(w_second.shape, BF),
            pltpu.VMEM(w_third.shape, BF),
            pltpu.VMEM(w_final.shape, BF),
            pltpu.VMEM((1, hid), F32),
            pltpu.VMEM((1, hid), F32),
            pltpu.VMEM((1, hid), F32),
            pltpu.VMEM((1, 2 * chans), F32),
            pltpu.VMEM((slots, 2 * chans), BF),
            pltpu.VMEM((owners, chans, cap), BF),
            pltpu.SMEM((2 * owners,), jnp.int32),
            pltpu.SemaphoreType.DMA((chunks,)),
            pltpu.SemaphoreType.DMA((chunks,)),
            pltpu.SemaphoreType.DMA((chunks,)),
            pltpu.SemaphoreType.DMA((5,)),
            pltpu.SemaphoreType.DMA((10,)),
            pltpu.SemaphoreType.DMA((2,)),
            pltpu.SemaphoreType.DMA((2,)),
        ],
        compiler_params=pltpu.CompilerParams(vmem_limit_bytes=60 << 20),
        cost_estimate=pl.CostEstimate(flops=10_000_000_000, bytes_accessed=8_000_000, transcendentals=12_000_000),
        name="columns",
    )(
        src, s, left, right, top, bot, f, cw, w_first, b_first.reshape(1, hid), w_second,
        b_second.reshape(1, hid), w_third, b_third.reshape(1, hid), w_final,
        b_final.reshape(1, 2 * chans),
    )
    got = lax.all_to_all(send, "lon", split_axis=0, concat_axis=0, tiled=True)
    new_state = pl.pallas_call(
        place_kernel,
        out_shape=jax.ShapeDtypeStruct((chans, rows, cols), BF),
        in_specs=[smem, hbm, hbm],
        out_specs=vmem,
        scratch_shapes=[
            pltpu.VMEM((cells + 8, 2 * chans), F32),
            pltpu.VMEM((LANES, 2 * chans), F32),
            pltpu.VMEM(tile_all, BF),
            pltpu.VMEM((slots, 2 * chans), BF),
            pltpu.VMEM((cols // LANES, chans * PITCH, LANES), F32),
            pltpu.SemaphoreType.DMA((2,)),
        ],
        compiler_params=pltpu.CompilerParams(vmem_limit_bytes=60 << 20),
        cost_estimate=pl.CostEstimate(flops=5_000_000_000, bytes_accessed=8_000_000, transcendentals=0),
        name="place",
    )(src, dyn, tend)
    owned = pl.pallas_call(
        owned_kernel,
        out_shape=jax.ShapeDtypeStruct((chans, owners, cap), BF),
        in_specs=[vmem],
        out_specs=vmem,
        scratch_shapes=[pltpu.VMEM((cap // LANES, chans * (owners + 1), LANES), F32)],
        compiler_params=pltpu.CompilerParams(vmem_limit_bytes=16 << 20),
        name="owned",
    )(got)
    return (new_state, owned.reshape(chans, 1, 1, owners, cap))


def solution(mesh):
    field = P(None, "lat", "lon")
    return jax.shard_map(
        body,
        mesh=mesh,
        in_specs=(field, field) + (P(),) * 9 + (P("lat", "lon"),) * 3 + (P("lat", "lon", None),),
        out_specs=(field, P(None, "lat", "lon", None, None)),
        check_vma=False,
    )
```
